512 devices in a mesh: ctx: 64 (over z, y), head: 8 (over x, core).
Axes of the slice: x: 4, y: 4, z: 16, core: 2. Of those that a mesh axis runs over, the one named last changes fastest.
Arguments:
- normalized_layer_input: bfloat16 [8192, 5120], P('ctx', 'head'), may hold values from -6 to 6
- queries: bfloat16 [8192, 8192], P('ctx', 'head'), may hold values from -40 to 40
- projected_keys: bfloat16 [8192, 1024], P('ctx', 'head'), may hold values from -9 to 9
- projected_values: bfloat16 [8192, 1024], P('ctx', 'head'), may hold values from -6 to 6
- frozen_path_gradient: bfloat16 [8192, 8192], P('ctx', 'head'), may hold values from -6 to 6
- output_gradient: bfloat16 [8192, 5120], P('ctx', 'head'), may hold values from -6 to 6
- document_length_list: int32 [128], replicated, may hold values from 1 to 1921, as said below
- query_down_adapter: bfloat16 [5120, 16], P('head'), may hold values from -0.078125 to 0.078125
- query_up_adapter: bfloat16 [16, 8192], P(None, 'head'), may hold values from -1.5 to 1.5
- key_down_adapter: bfloat16 [5120, 16], P('head'), may hold values from -0.078125 to 0.078125
- key_up_adapter: bfloat16 [16, 1024], P(None, 'head'), may hold values from -1.5 to 1.5
- value_down_adapter: bfloat16 [5120, 16], P('head'), may hold values from -0.078125 to 0.078125
- value_up_adapter: bfloat16 [16, 1024], P(None, 'head'), may hold values from -1.5 to 1.5
- output_down_adapter: bfloat16 [8192, 16], P('head'), may hold values from -0.0625 to 0.0625
- output_up_adapter: bfloat16 [16, 5120], P(None, 'head'), may hold values from -1.5 to 1.5
Outputs:
- query_gradient: bfloat16 [8192, 8192], P('ctx', 'head')
- key_gradient: bfloat16 [8192, 1024], P('ctx', 'head')
- value_gradient: bfloat16 [8192, 1024], P('ctx', 'head')
- query_down_gradient: float32 [5120, 16], P('head')
- query_up_gradient: float32 [16, 8192], P(None, 'head')
- key_down_gradient: float32 [5120, 16], P('head')
- key_up_gradient: float32 [16, 1024], P(None, 'head')
- value_down_gradient: float32 [5120, 16], P('head')
- value_up_gradient: float32 [16, 1024], P(None, 'head')
- output_down_gradient: float32 [8192, 16], P('head')
- output_up_gradient: float32 [16, 5120], P(None, 'head')
The draws below stay inside these ranges and needn't reach their ends.
Inputs may be any that keep to these rules, and one draw needn't show every extreme that they name: `document_length_list`: they sum to 8192; exactly two of them, at places in the list that vary from draw to draw, have 1921 tokens.
All inputs are finite; a program needn't handle non-finite values.
Results may differ from the reference program's by a relative error of at most 0.015.
Values may be sent and summed in bfloat16 or wider, within the bound.
No kernel may reach another device: no remote copies, remote signals or barrier semaphores. Data moves between devices by JAX's collectives and lax.ppermute only.
A program may use at most 64 MiB of HBM per device.

```python
import jax
import jax.numpy as jnp
from jax import lax

MODEL_WIDTH = 5120
QUERY_HEADS = 64
KEY_VALUE_HEADS = 8
HEAD_SIZE = 128
ADAPTER_RANK = 16
TOK_DEV = 128
TOKENS = 8192
SPAN = 16
MAXDOC = 1921
NDOCS = 128
N_CTX = 64


def shared_keys(key):
    return jax.random.normal(key, (TOKENS, KEY_VALUE_HEADS * HEAD_SIZE), jnp.float32)


def draw_projected_keys(key, part):
    base_keys = shared_keys(key)
    return jnp.clip(base_keys, -6.0, 6.0).astype(jnp.bfloat16)


def draw_queries(key, part):
    key = jax.random.fold_in(key, 23)
    fresh_key = jax.random.fold_in(key, 0)
    fresh = jax.random.normal(fresh_key, (TOKENS, QUERY_HEADS * HEAD_SIZE), jnp.float32)
    return jnp.clip(fresh, -6.0, 6.0).astype(jnp.bfloat16)


def draw_document_length_list(key, part):
    key = jax.random.fold_in(key, 37)
    jitter_key, place_key = jax.random.split(key)
    short_count = NDOCS - 2
    remaining = TOKENS - 2 * MAXDOC
    stride = remaining // short_count
    jitter = jax.random.randint(jitter_key, (short_count - 1,), 0, stride, dtype=jnp.int32)
    cuts = jnp.arange(1, short_count, dtype=jnp.int32) * stride + jitter
    bounds = jnp.concatenate([jnp.zeros((1,), jnp.int32), cuts, jnp.full((1,), remaining, jnp.int32)])
    pieces = bounds[1:] - bounds[:-1]
    order = jax.random.permutation(place_key, NDOCS).astype(jnp.int32)
    first_long = jnp.minimum(order[0], order[1])
    second_long = jnp.maximum(order[0], order[1])
    slots = jnp.arange(NDOCS, dtype=jnp.int32)
    longs_before = (slots > first_long).astype(jnp.int32) + (slots > second_long).astype(jnp.int32)
    short_index = jnp.clip(slots - longs_before, 0, short_count - 1).astype(jnp.int32)
    short_here = jnp.take(pieces, short_index)
    is_long = (slots == first_long) | (slots == second_long)
    return jnp.where(is_long, jnp.int32(MAXDOC), short_here).astype(jnp.int32)


def block_levels(stream_key, shape, shards, low, top_value):
    loudness, own = 1.0, jax.random.fold_in(stream_key, 6)
    for position, shards_of in shards:
        heights = jnp.exp(jax.random.uniform(jax.random.fold_in(own, position), (shards_of,), jnp.float32, low / len(shards), top_value / len(shards)))
        loudness = loudness * jnp.repeat(heights, shape[position] // shards_of).reshape([-1 if axis == position else 1 for axis in range(len(shape))])
    return loudness


def scatter_about(rng, dims, deviation, most, cuts=(), held_as=jnp.bfloat16):
    values = deviation * jax.random.normal(rng, dims, jnp.float32)
    if cuts:
        values = values * block_levels(rng, dims, cuts, -0.22, 0.18)
    return jnp.clip(values, -most, most).astype(held_as)


def setup_inputs(seed: int = 0) -> dict:
    splits = jax.random.split(jax.random.key(seed), 16)
    return {
        "normalized_layer_input": scatter_about(splits[0], (TOKENS, MODEL_WIDTH), 1.0, 6.0, ((0, 64), (1, 8))),
        "queries": draw_queries(jax.random.fold_in(splits[15], 71), 0),
        "projected_keys": draw_projected_keys(jax.random.fold_in(splits[15], 71), 0),
        "projected_values": scatter_about(splits[3], (TOKENS, KEY_VALUE_HEADS * HEAD_SIZE), 1.0, 6.0, ((0, 64), (1, 8))),
        "frozen_path_gradient": scatter_about(splits[4], (TOKENS, QUERY_HEADS * HEAD_SIZE), 1.0, 6.0, ((0, 64), (1, 8))),
        "output_gradient": scatter_about(splits[5], (TOKENS, MODEL_WIDTH), 1.0, 6.0, ((0, 64), (1, 8))),
        "document_length_list": draw_document_length_list(jax.random.fold_in(splits[15], 71), 0),
        "query_down_adapter": scatter_about(splits[7], (MODEL_WIDTH, ADAPTER_RANK), MODEL_WIDTH ** -0.5, 0.078125, ((0, 8),)),
        "query_up_adapter": scatter_about(splits[8], (ADAPTER_RANK, QUERY_HEADS * HEAD_SIZE), ADAPTER_RANK ** -0.5, 1.5, ((1, 8),)),
        "key_down_adapter": scatter_about(splits[9], (MODEL_WIDTH, ADAPTER_RANK), MODEL_WIDTH ** -0.5, 0.078125, ((0, 8),)),
        "key_up_adapter": scatter_about(splits[10], (ADAPTER_RANK, KEY_VALUE_HEADS * HEAD_SIZE), ADAPTER_RANK ** -0.5, 1.5, ((1, 8),)),
        "value_down_adapter": scatter_about(splits[11], (MODEL_WIDTH, ADAPTER_RANK), MODEL_WIDTH ** -0.5, 0.078125, ((0, 8),)),
        "value_up_adapter": scatter_about(splits[12], (ADAPTER_RANK, KEY_VALUE_HEADS * HEAD_SIZE), ADAPTER_RANK ** -0.5, 1.5, ((1, 8),)),
        "output_down_adapter": scatter_about(splits[13], (QUERY_HEADS * HEAD_SIZE, ADAPTER_RANK), (QUERY_HEADS * HEAD_SIZE) ** -0.5, 0.0625, ((0, 8),)),
        "output_up_adapter": scatter_about(splits[14], (ADAPTER_RANK, MODEL_WIDTH), ADAPTER_RANK ** -0.5, 1.5, ((1, 8),)),
    }


ADAPTER_SCALE = 2.0
NEG = -1.0e30


def doc_index(positions, doc_ends):
    found = jnp.sum((positions[:, None] >= doc_ends[None, :]).astype(jnp.int32), axis=1)
    return jnp.where(positions >= 0, found, -1)


def rounded(tensor):
    return lax.optimization_barrier(tensor.astype(jnp.bfloat16)).astype(jnp.float32)


def reference(normalized_layer_input, queries, projected_keys, projected_values, frozen_path_gradient, output_gradient, document_length_list, query_down_adapter, query_up_adapter, key_down_adapter, key_up_adapter, value_down_adapter, value_up_adapter, output_down_adapter, output_up_adapter):
    group_size = QUERY_HEADS // KEY_VALUE_HEADS
    margin = (SPAN - 1) * TOK_DEV
    window = SPAN * TOK_DEV
    score_scale = HEAD_SIZE ** -0.5
    query_down_product = jnp.dot(normalized_layer_input, query_down_adapter, preferred_element_type=jnp.float32).astype(jnp.bfloat16)
    key_down_product = jnp.dot(normalized_layer_input, key_down_adapter, preferred_element_type=jnp.float32).astype(jnp.bfloat16)
    value_down_product = jnp.dot(normalized_layer_input, value_down_adapter, preferred_element_type=jnp.float32).astype(jnp.bfloat16)
    output_down_product = jnp.dot(output_gradient, output_up_adapter.T, preferred_element_type=jnp.float32).astype(jnp.bfloat16)
    per_head_gradient = (frozen_path_gradient.astype(jnp.float32) + ADAPTER_SCALE * jnp.dot(output_down_product, output_down_adapter.T, preferred_element_type=jnp.float32)).astype(jnp.bfloat16)
    key_pad = jnp.concatenate([jnp.zeros((margin, KEY_VALUE_HEADS * HEAD_SIZE), jnp.bfloat16), projected_keys], axis=0).reshape(margin + TOKENS, KEY_VALUE_HEADS, HEAD_SIZE)
    value_pad = jnp.concatenate([jnp.zeros((margin, KEY_VALUE_HEADS * HEAD_SIZE), jnp.bfloat16), projected_values], axis=0).reshape(margin + TOKENS, KEY_VALUE_HEADS, HEAD_SIZE)
    query_four = queries.reshape(TOKENS, KEY_VALUE_HEADS, group_size, HEAD_SIZE)
    grad_four = per_head_gradient.reshape(TOKENS, KEY_VALUE_HEADS, group_size, HEAD_SIZE)
    doc_ends = jnp.cumsum(document_length_list, dtype=jnp.int32)
    offsets = jnp.arange(TOK_DEV, dtype=jnp.int32)
    wide_offsets = jnp.arange(window, dtype=jnp.int32)

    def visit(sums, block_idx):
        grad_keys, grad_values = sums
        start = block_idx * TOK_DEV
        q_pos = start + offsets
        k_pos = start - margin + wide_offsets
        allowed = (doc_index(k_pos, doc_ends)[None, :] == doc_index(q_pos, doc_ends)[:, None]) & (k_pos[None, :] <= q_pos[:, None])
        q_blk = lax.dynamic_slice_in_dim(query_four, start, TOK_DEV, 0).astype(jnp.float32)
        g_blk = lax.dynamic_slice_in_dim(grad_four, start, TOK_DEV, 0).astype(jnp.float32)
        k_blk = lax.dynamic_slice_in_dim(key_pad, start, window, 0).astype(jnp.float32)
        v_blk = lax.dynamic_slice_in_dim(value_pad, start, window, 0).astype(jnp.float32)
        raw_scores = jnp.einsum("qhgd,khd->hgqk", q_blk, k_blk) * score_scale
        masked = jnp.where(allowed, raw_scores, NEG)
        row_top = jnp.max(masked, axis=-1)
        weights = jnp.where(allowed, jnp.exp(masked - row_top[..., None]), 0.0)
        row_total = jnp.sum(weights, axis=-1)
        log_norm = row_top + jnp.log(row_total)
        weighted = jnp.einsum("hgqk,khd->hgqd", weights, v_blk, precision=lax.Precision.HIGHEST)
        attention_output = (weighted / row_total[..., None]).transpose(2, 0, 1, 3).astype(jnp.bfloat16)
        row_delta = jnp.einsum("qhgd,qhgd->hgq", g_blk, attention_output.astype(jnp.float32))
        attn_prob = jnp.where(allowed, jnp.exp(masked - log_norm[..., None]), 0.0)
        grad_prob = jnp.einsum("qhgd,khd->hgqk", g_blk, v_blk)
        grad_score = rounded(attn_prob * (grad_prob - row_delta[..., None]))
        prob_low = rounded(attn_prob)
        grad_q = jnp.einsum("hgqk,khd->qhgd", grad_score, k_blk) * score_scale
        grad_k = jnp.einsum("hgqk,qhgd->khd", grad_score, q_blk) * score_scale
        grad_v = jnp.einsum("hgqk,qhgd->khd", prob_low, g_blk)
        grad_keys = lax.dynamic_update_slice_in_dim(grad_keys, lax.dynamic_slice_in_dim(grad_keys, start, window, 0) + grad_k, start, 0)
        grad_values = lax.dynamic_update_slice_in_dim(grad_values, lax.dynamic_slice_in_dim(grad_values, start, window, 0) + grad_v, start, 0)
        return (grad_keys, grad_values), (attention_output, grad_q.astype(jnp.bfloat16))

    zero_sums = jnp.zeros((margin + TOKENS, KEY_VALUE_HEADS, HEAD_SIZE), jnp.float32)
    (grad_keys, grad_values), (outs_all, grads_all) = lax.scan(visit, (zero_sums, zero_sums), jnp.arange(N_CTX, dtype=jnp.int32))
    attention_full = outs_all.reshape(TOKENS, QUERY_HEADS * HEAD_SIZE)
    query_gradient = grads_all.reshape(TOKENS, QUERY_HEADS * HEAD_SIZE)
    key_gradient = grad_keys[margin:].reshape(TOKENS, KEY_VALUE_HEADS * HEAD_SIZE).astype(jnp.bfloat16)
    value_gradient = grad_values[margin:].reshape(TOKENS, KEY_VALUE_HEADS * HEAD_SIZE).astype(jnp.bfloat16)
    output_adapter_term = jnp.dot(attention_full, output_down_adapter, preferred_element_type=jnp.float32).astype(jnp.bfloat16)
    query_backward = jnp.dot(query_gradient, query_up_adapter.T, preferred_element_type=jnp.float32).astype(jnp.bfloat16)
    key_backward = jnp.dot(key_gradient, key_up_adapter.T, preferred_element_type=jnp.float32).astype(jnp.bfloat16)
    value_backward = jnp.dot(value_gradient, value_up_adapter.T, preferred_element_type=jnp.float32).astype(jnp.bfloat16)
    query_down_gradient = ADAPTER_SCALE * jnp.dot(normalized_layer_input.T, query_backward, preferred_element_type=jnp.float32)
    query_up_gradient = ADAPTER_SCALE * jnp.dot(query_down_product.T, query_gradient, preferred_element_type=jnp.float32)
    key_down_gradient = ADAPTER_SCALE * jnp.dot(normalized_layer_input.T, key_backward, preferred_element_type=jnp.float32)
    key_up_gradient = ADAPTER_SCALE * jnp.dot(key_down_product.T, key_gradient, preferred_element_type=jnp.float32)
    value_down_gradient = ADAPTER_SCALE * jnp.dot(normalized_layer_input.T, value_backward, preferred_element_type=jnp.float32)
    value_up_gradient = ADAPTER_SCALE * jnp.dot(value_down_product.T, value_gradient, preferred_element_type=jnp.float32)
    output_down_gradient = ADAPTER_SCALE * jnp.dot(attention_full.T, output_down_product, preferred_element_type=jnp.float32)
    output_up_gradient = ADAPTER_SCALE * jnp.dot(output_adapter_term.T, output_gradient, preferred_element_type=jnp.float32)
    return (query_gradient, key_gradient, value_gradient, query_down_gradient, query_up_gradient, key_down_gradient, key_up_gradient, value_down_gradient, value_up_gradient, output_down_gradient, output_up_gradient)
```

```python
import functools

import jax
import jax.numpy as jnp
from jax import lax
from jax.experimental import pallas as pl
from jax.experimental.pallas import tpu as pltpu
from jax.sharding import PartitionSpec as P

HEAD = 128
ROWS = 128
GROUP = 8
RANK = 16
TILES = 40
SCALE = HEAD**-0.5
LOG2E = 1.4426950408889634
ADAPTER_SCALE = 2.0
NEG = -1e30
F32 = jnp.float32
BF16 = jnp.bfloat16

Y_GROUPS = [[4 * z + y for y in range(4)] for z in range(16)]
Z_FOURS = [[16 * zh + 4 * k + y for k in range(4)] for zh in range(4) for y in range(4)]
EIGHTS = [[8 * g + i for i in range(8)] for g in range(8)]
STRIDED = [[g + 8 * i for i in range(8)] for g in range(8)]


def nn(a, b):
    return lax.dot_general(a, b, (((1,), (0,)), ((), ())), preferred_element_type=F32)


def nt(a, b):
    return lax.dot_general(a, b, (((1,), (1,)), ((), ())), preferred_element_type=F32)


def tn(a, b):
    return lax.dot_general(a, b, (((0,), (0,)), ((), ())), preferred_element_type=F32)


def call(body, outs, *args, scratch=(), vmem=32, flops=1 << 20):
    return pl.pallas_call(
        body,
        out_shape=outs,
        in_specs=[pl.BlockSpec(memory_space=pltpu.VMEM)] * len(args),
        out_specs=jax.tree.map(lambda _: pl.BlockSpec(memory_space=pltpu.VMEM), outs),
        scratch_shapes=list(scratch),
        compiler_params=pltpu.CompilerParams(vmem_limit_bytes=vmem << 20),
        cost_estimate=pl.CostEstimate(flops=flops, bytes_accessed=1 << 20, transcendentals=0),
    )(*args)


def shaped(shape, dtype):
    return jax.ShapeDtypeStruct(shape, dtype)


def project_kernel(x_ref, dout_ref, qd_ref, kd_ref, vd_ref, ou_ref, out_ref, wide):
    wide[:, 0:16] = nn(x_ref[...], qd_ref[...])
    wide[:, 16:32] = nn(x_ref[...], kd_ref[...])
    wide[:, 32:48] = nn(x_ref[...], vd_ref[...])
    wide[:, 48:64] = nt(dout_ref[...], ou_ref[...])
    low = wide[...].T.astype(BF16)
    for peer in range(8):
        out_ref[peer] = low[:64]


def spread_z_kernel(own_ref, far_ref, out_ref):
    place = (lax.axis_index("ctx") // 4) % 4
    for dest in range(4):

        @pl.when(dest >= place)
        def _(dest=dest):
            out_ref[dest] = own_ref[...]

        @pl.when(dest < place)
        def _(dest=dest):
            out_ref[dest] = far_ref[...]


def spread_y_kernel(z_ref, far_ref, out_ref):
    index = lax.axis_index("ctx")
    place, y = (index // 4) % 4, index % 4
    for dest in range(4):
        out_ref[dest] = z_ref[...]

        @pl.when(dest < y)
        def _(dest=dest):
            out_ref[dest, place] = far_ref[...]


def gradient_kernel(f_ref, low_ref, od_ref, g_ref, sum_ref):
    low = low_ref[0].astype(F32)
    for peer in range(1, 8):
        low = low + low_ref[peer].astype(F32)
    sum_ref[...] = low
    u = low[48:64].T.astype(BF16)
    for n in range(GROUP):
        cols = slice(n * HEAD, (n + 1) * HEAD)
        g_n = f_ref[:, cols].astype(F32) + ADAPTER_SCALE * nt(u, od_ref[cols, :])
        g_ref[:, cols] = g_n.astype(BF16)


def attention_kernel(
    q_ref, g_ref, low_ref, od_ref, qu_ref, kv_ref, len_ref,
    dq_ref, dkv_ref, back_ref, tot_ref,
    qs, qt, gs, gt, s_ref, ot, dqt, dk, dv, bias, top, total, delta,
):
    index = lax.axis_index("ctx")
    here = index % 16
    xa_q = low_ref[0:16].astype(BF16)
    u_t = low_ref[48:64].astype(BF16)
    doc = lax.broadcasted_iota(jnp.int32, (128, 128), 0)
    lane = lax.broadcasted_iota(jnp.int32, (128, 128), 1)
    lengths = jnp.broadcast_to(len_ref[...].astype(F32), (128, 128))
    ends = jnp.sum(jnp.where(lane <= doc, lengths, 0.0), axis=1, keepdims=True)
    position = (lane + index * ROWS).astype(F32)
    start = jnp.max(jnp.where(ends <= position, ends, 0.0), axis=0, keepdims=True)
    first = jnp.min(start).astype(jnp.int32)
    reach = jnp.maximum(index * ROWS - first + ROWS - 1, 0) // ROWS
    start = start.astype(jnp.int32)
    q_pos = lax.broadcasted_iota(jnp.int32, (1, 128), 1) + index * ROWS
    for n in range(GROUP):
        cols = slice(n * HEAD, (n + 1) * HEAD)
        q_n = q_ref[:, cols]
        qs[cols, :] = q_n
        qt[:, cols] = q_n.T
        g_n = g_ref[:, cols]
        gs[cols, :] = g_n
        gt[:, cols] = g_n.T
    top[...] = jnp.full_like(top, NEG)
    total[...] = jnp.zeros_like(total)
    ot[...] = jnp.zeros_like(ot)
    dqt[...] = jnp.zeros_like(dqt)

    def live(plane):
        nearest = jnp.minimum(
            jnp.minimum((here - 4 * plane) & 15, (here - 4 * plane - 1) & 15),
            jnp.minimum((here - 4 * plane - 2) & 15, (here - 4 * plane - 3) & 15),
        )
        return nearest <= reach

    pairs = [slice(256 * p, 256 * (p + 1)) for p in range(4)]

    def keys(plane, which):
        return kv_ref[:, plane, which].reshape(512, HEAD)

    def scores(plane, _):
        @pl.when(live(plane))
        def _():
            for y in range(4):
                back = (here - 4 * plane - y) & 15
                k_pos = lax.broadcasted_iota(jnp.int32, (128, 128), 0) + (index - back) * ROWS
                bias[y * 128 : (y + 1) * 128, :] = jnp.where(
                    (k_pos >= start) & (k_pos <= q_pos), 0.0, NEG
                )
            key_quad = keys(plane, 0)
            for cols in pairs:
                raw = nn(key_quad, qt[:, cols])
                wide_bias = jnp.concatenate([bias[...], bias[...]], axis=1)
                raw = raw * (SCALE * LOG2E) + wide_bias
                s_ref[plane, :, cols] = raw
                top[:, cols] = jnp.maximum(top[:, cols], jnp.max(raw, axis=0, keepdims=True))

        return 0

    lax.fori_loop(0, 4, scores, 0)

    def weigh(plane, _):
        @pl.when(live(plane))
        def _():
            value_quad = keys(plane, 1)
            for cols in pairs:
                prob = jnp.exp2(s_ref[plane, :, cols] - top[:, cols])
                s_ref[plane, :, cols] = prob
                total[:, cols] += jnp.sum(prob, axis=0, keepdims=True)
                ot[:, cols] += tn(value_quad, prob.astype(BF16))

        return 0

    lax.fori_loop(0, 4, weigh, 0)
    total[...] = 1.0 / total[...]
    for n in range(GROUP):
        cols = slice(n * HEAD, (n + 1) * HEAD)
        o_n = (ot[:, cols] * total[:, cols]).astype(BF16)
        delta[:, cols] = jnp.sum(
            o_n.astype(F32) * gt[:, cols].astype(F32), axis=0, keepdims=True
        )

    def grads(plane, _):
        @pl.when(live(plane))
        def _():
            key_quad = keys(plane, 0)
            value_quad = keys(plane, 1)
            for p, cols in enumerate(pairs):
                prob = s_ref[plane, :, cols] * total[:, cols]
                grad_prob = nn(value_quad, gt[:, cols])
                grad_score = (prob * (grad_prob - delta[:, cols])).astype(BF16)
                dqt[:, cols] += tn(key_quad, grad_score)
                part_k = nn(grad_score, qs[cols, :])
                part_v = nn(prob.astype(BF16), gs[cols, :])
                if p == 0:
                    dk[...] = part_k
                    dv[...] = part_v
                else:
                    dk[...] += part_k
                    dv[...] += part_v
            dkv_ref[:, plane, 0] = (dk[...] * SCALE).astype(BF16).reshape(4, 128, HEAD)
            dkv_ref[:, plane, 1] = dv[...].astype(BF16).reshape(4, 128, HEAD)

        @pl.when(jnp.logical_not(live(plane)))
        def _():
            for y in range(4):
                dkv_ref[y, plane] = jnp.zeros((2, 128, HEAD), BF16)

        return 0

    lax.fori_loop(0, 4, grads, 0)
    out_adapter = jnp.zeros((RANK, ROWS), F32)
    back_q = jnp.zeros((RANK, ROWS), F32)
    for n in range(GROUP):
        cols = slice(n * HEAD, (n + 1) * HEAD)
        dq_t = (dqt[:, cols] * SCALE).astype(BF16)
        dq_n = dq_t.T
        dq_ref[:, cols] = dq_n
        back_q = back_q + nn(qu_ref[:, cols], dq_t)
        tot_ref[GROUP + n] = (ADAPTER_SCALE * nn(xa_q, dq_n)).astype(BF16)
        o_n = (ot[:, cols] * total[:, cols]).astype(BF16)
        out_adapter = out_adapter + tn(od_ref[cols, :], o_n)
        tot_ref[n] = (ADAPTER_SCALE * nt(u_t, o_n)).astype(BF16)
    back_ref[0:16] = out_adapter
    back_ref[16:32] = back_q
    back_ref[32:64] = low_ref[16:48]


def gather_y_kernel(y_ref, out_ref, far_ref):
    index = lax.axis_index("ctx")
    place, y = (index // 4) % 4, index % 4
    for plane in range(4):
        acc = y_ref[0, plane].astype(F32)
        for source in range(1, 4):
            acc = acc + y_ref[source, plane].astype(F32)
        out_ref[plane] = acc.astype(BF16)
    mine = jnp.zeros((2, 128, HEAD), F32)
    far = jnp.zeros((2, 128, HEAD), F32)
    for source in range(4):
        term = y_ref[source, place].astype(F32)
        keep = (source >= y).astype(F32)
        mine = mine + term * keep
        far = far + term * (1.0 - keep)
    out_ref[place] = mine.astype(BF16)
    far_ref[...] = far


def gather_z_kernel(z_ref, far_ref, own_ref, send_ref):
    place = (lax.axis_index("ctx") // 4) % 4
    mine = jnp.zeros((2, 128, HEAD), F32)
    far = far_ref[...]
    for source in range(4):
        term = z_ref[source].astype(F32)
        keep = (source >= place).astype(F32)
        mine = mine + term * keep
        far = far + term * (1.0 - keep)
    own_ref[...] = mine
    send_ref[...] = far.astype(BF16)


def owner_kernel(own_ref, far_ref, back_ref, ku_ref, vu_ref, dk_ref, dv_ref, out_ref, tot_ref):
    d_k = (own_ref[0] + far_ref[0].astype(F32)).astype(BF16)
    d_v = (own_ref[1] + far_ref[1].astype(F32)).astype(BF16)
    dk_ref[...] = d_k
    dv_ref[...] = d_v
    xa_k = back_ref[32:48].astype(BF16)
    xa_v = back_ref[48:64].astype(BF16)
    tot_ref[0] = (ADAPTER_SCALE * nn(xa_k, d_k)).astype(BF16)
    tot_ref[1] = (ADAPTER_SCALE * nn(xa_v, d_v)).astype(BF16)
    back_k = nt(ku_ref[...], d_k)
    back_v = nt(vu_ref[...], d_v)
    sent = jnp.concatenate([back_ref[0:32], back_k, back_v], axis=0).astype(BF16)
    for peer in range(8):
        out_ref[peer] = sent


def down_kernel(low_ref, x_ref, dout_ref, tot_ref, kv_tot_ref, out_ref):
    low = low_ref[0].astype(F32)
    for peer in range(1, 8):
        low = low + low_ref[peer].astype(F32)
    low = low.astype(BF16)
    down = (ADAPTER_SCALE * nn(low[16:64], x_ref[...])).astype(BF16)
    up = (ADAPTER_SCALE * nn(low[0:16], dout_ref[...])).astype(BF16)
    tiles = []
    for which in range(3):
        for t in range(5):
            tiles.append(down[which * 16 : (which + 1) * 16, t * 128 : (t + 1) * 128])
    for t in range(5):
        tiles.append(up[:, t * 128 : (t + 1) * 128])
    for t in range(16):
        tiles.append(tot_ref[t])
    tiles.append(kv_tot_ref[0])
    tiles.append(kv_tot_ref[1])
    zero = jnp.zeros((16, 128), BF16)
    tiles += [zero, zero]
    for t, tile in enumerate(tiles):
        out_ref[t // 5, t % 5] = tile


def sum_spread_kernel(in_ref, out_ref):
    acc = in_ref[0].astype(F32)
    for peer in range(1, 8):
        acc = acc + in_ref[peer].astype(F32)
    acc = acc.astype(BF16)
    for peer in range(8):
        out_ref[peer] = acc


def unpack_kernel(in_ref, qd_ref, qu_ref, kd_ref, ku_ref, vd_ref, vu_ref, od_ref, ou_ref):
    def tile(t):
        return in_ref[t // 5, t % 5].astype(F32)

    for which, ref in enumerate((qd_ref, kd_ref, vd_ref)):
        for t in range(5):
            ref[t * 128 : (t + 1) * 128, :] = tile(which * 5 + t).T
    for t in range(5):
        ou_ref[:, t * 128 : (t + 1) * 128] = tile(15 + t)
    for t in range(8):
        od_ref[t * 128 : (t + 1) * 128, :] = tile(20 + t).T
        qu_ref[:, t * 128 : (t + 1) * 128] = tile(28 + t)
    ku_ref[...] = tile(36)
    vu_ref[...] = tile(37)


def shift(value, steps):
    count = lax.axis_size("ctx")
    first, last = max(0, -steps), min(count, count - steps)
    return lax.ppermute(value, "ctx", [(i, i + steps) for i in range(first, last)])


def exchange(value, groups):
    return lax.all_to_all(value, "ctx", 0, 0, tiled=True, axis_index_groups=groups)


def exchange_head(value):
    return lax.all_to_all(value, "head", 0, 0, tiled=True)


def shards(x, q, keys, values, frozen, dout, lengths, qd, qu, kd, ku, vd, vu, od, ou):
    pair = jnp.stack([keys, values])
    far = shift(pair, 16)
    low = call(
        project_kernel, shaped((8, 64, 128), BF16), x, dout, qd, kd, vd, ou,
        scratch=[pltpu.VMEM((128, 128), F32)],
    )
    grad_heads, low = call(
        gradient_kernel,
        (shaped((128, 1024), BF16), shaped((64, 128), F32)),
        frozen, exchange_head(low), od,
    )
    by_z = exchange(call(spread_z_kernel, shaped((4, 2, 128, 128), BF16), pair, far), Z_FOURS)
    window = call(spread_y_kernel, shaped((4, 4, 2, 128, 128), BF16), by_z, far)
    window = exchange(window, Y_GROUPS)
    dq, dkv, back, totals = call(
        attention_kernel,
        (
            shaped((128, 1024), BF16),
            shaped((4, 4, 2, 128, 128), BF16),
            shaped((64, 128), F32),
            shaped((16, 16, 128), BF16),
        ),
        q, grad_heads, low, od, qu, window, lengths.reshape(1, 128),
        scratch=[
            pltpu.VMEM((1024, 128), BF16),
            pltpu.VMEM((128, 1024), BF16),
            pltpu.VMEM((1024, 128), BF16),
            pltpu.VMEM((128, 1024), BF16),
            pltpu.VMEM((4, 512, 1024), F32),
            pltpu.VMEM((128, 1024), F32),
            pltpu.VMEM((128, 1024), F32),
            pltpu.VMEM((512, 128), F32),
            pltpu.VMEM((512, 128), F32),
            pltpu.VMEM((512, 128), F32),
            pltpu.VMEM((1, 1024), F32),
            pltpu.VMEM((1, 1024), F32),
            pltpu.VMEM((1, 1024), F32),
        ],
        vmem=48,
        flops=3 << 30,
    )
    dkv = exchange(dkv, Y_GROUPS)
    dkv, far_sum = call(
        gather_y_kernel, (shaped((4, 2, 128, 128), BF16), shaped((2, 128, 128), F32)), dkv
    )
    dkv = exchange(dkv, Z_FOURS)
    own, far_send = call(
        gather_z_kernel,
        (shaped((2, 128, 128), F32), shaped((2, 128, 128), BF16)),
        dkv, far_sum,
    )
    arrived = shift(far_send, -16)
    dk, dv, low_back, kv_totals = call(
        owner_kernel,
        (
            shaped((128, 128), BF16),
            shaped((128, 128), BF16),
            shaped((8, 64, 128), BF16),
            shaped((2, 16, 128), BF16),
        ),
        own, arrived, back, ku, vu,
    )
    low_back = exchange_head(low_back)
    packed = shaped((8, 5, 16, 128), BF16)
    sums = call(down_kernel, packed, low_back, x, dout, totals, kv_totals)
    sums = call(sum_spread_kernel, packed, exchange(sums, EIGHTS))
    sums = call(sum_spread_kernel, packed, exchange(sums, STRIDED))
    sums = exchange(sums, EIGHTS)
    grads = call(
        unpack_kernel,
        (
            shaped((640, 16), F32),
            shaped((16, 1024), F32),
            shaped((640, 16), F32),
            shaped((16, 128), F32),
            shaped((640, 16), F32),
            shaped((16, 128), F32),
            shaped((1024, 16), F32),
            shaped((16, 640), F32),
        ),
        sums,
    )
    return (dq, dk, dv, *grads)


def solution(mesh):
    rows, cols, tokens = P("head", None), P(None, "head"), P("ctx", "head")
    return jax.shard_map(
        shards,
        mesh=mesh,
        in_specs=(tokens,) * 6 + (P(),) + (rows, cols) * 4,
        out_specs=(tokens,) * 3 + (rows, cols) * 4,
        check_vma=False,
    )
```

```python
import functools

import jax
import jax.numpy as jnp
from jax import lax
from jax.experimental import pallas as pl
from jax.experimental.pallas import tpu as pltpu
from jax.sharding import PartitionSpec as P

HEAD = 128
ROWS = 128
GROUP = 8
RANK = 16
TILES = 40
SCALE = HEAD**-0.5
LOG2E = 1.4426950408889634
ADAPTER_SCALE = 2.0
NEG = -1e30
F32 = jnp.float32
BF16 = jnp.bfloat16

Y_GROUPS = [[4 * z + y for y in range(4)] for z in range(16)]
EIGHTS = [[8 * g + i for i in range(8)] for g in range(8)]
STRIDED = [[g + 8 * i for i in range(8)] for g in range(8)]


def nn(a, b):
    return lax.dot_general(a, b, (((1,), (0,)), ((), ())), preferred_element_type=F32)


def nt(a, b):
    return lax.dot_general(a, b, (((1,), (1,)), ((), ())), preferred_element_type=F32)


def tn(a, b):
    return lax.dot_general(a, b, (((0,), (0,)), ((), ())), preferred_element_type=F32)


def call(body, outs, *args, scratch=(), vmem=32, flops=1 << 20):
    return pl.pallas_call(
        body,
        out_shape=outs,
        scratch_shapes=list(scratch),
        compiler_params=pltpu.CompilerParams(vmem_limit_bytes=vmem << 20),
        cost_estimate=pl.CostEstimate(flops=flops, bytes_accessed=1 << 20, transcendentals=0),
    )(*args)


def shaped(shape, dtype):
    return jax.ShapeDtypeStruct(shape, dtype)


def project_kernel(x_ref, dout_ref, qd_ref, kd_ref, vd_ref, ou_ref, out_ref):
    parts = [nt(ref[...], x_ref[...]) for ref in (qd_ref, kd_ref, vd_ref)]
    parts.append(nt(ou_ref[...], dout_ref[...]))
    low = jnp.concatenate(parts, axis=0).astype(BF16)
    for peer in range(8):
        out_ref[peer] = low


def spread_kernel(
    pair_ref, one_ref, two_ref, four_ref, low_ref, x_ref, out_ref, x_out, sum_ref
):
    y = lax.axis_index("ctx") % 4
    for dest in range(4):

        @pl.when(dest >= y)
        def _(dest=dest):
            out_ref[dest, 0] = pair_ref[...]

        @pl.when(dest < y)
        def _(dest=dest):
            out_ref[dest, 0] = four_ref[...]

        out_ref[dest, 1] = one_ref[...]
        out_ref[dest, 2] = two_ref[0]
        out_ref[dest, 3] = two_ref[1]
    low = low_ref[0].astype(F32)
    for peer in range(1, 8):
        low = low + low_ref[peer].astype(F32)
    low = low.astype(BF16)
    sum_ref[...] = low
    for t in range(5):
        x_out[t * 128 : (t + 1) * 128, :] = x_ref[:, t * 128 : (t + 1) * 128]
    x_out[640:672, :] = low[16:48]


def prepare_kernel(q_ref, f_ref, low_ref, od_ref, qs_ref, qt_ref, gs_ref, gt_ref):
    u = low_ref[48:64]
    for n in range(GROUP):
        cols = slice(n * HEAD, (n + 1) * HEAD)
        q_n = q_ref[:, cols]
        qs_ref[cols, :] = q_n
        qt_ref[:, cols] = q_n.T
        g_n = f_ref[:, cols].astype(F32) + ADAPTER_SCALE * tn(u, od_ref[:, cols])
        g_n = g_n.astype(BF16)
        gs_ref[cols, :] = g_n
        gt_ref[:, cols] = g_n.T


def attention_kernel(
    qs, qt, gs, gt, kv_ref, len_ref,
    dqt_ref, ot_ref, dkv_ref,
    s_ref, ot, dqt, dk, dv, bias, top, total, delta,
):
    index = lax.axis_index("ctx")
    y_place = index % 4
    doc = lax.broadcasted_iota(jnp.int32, (128, 128), 0)
    lane = lax.broadcasted_iota(jnp.int32, (128, 128), 1)
    lengths = jnp.broadcast_to(len_ref[...].astype(F32), (128, 128))
    ends = jnp.sum(jnp.where(lane <= doc, lengths, 0.0), axis=1, keepdims=True)
    position = (lane + index * ROWS).astype(F32)
    start = jnp.max(jnp.where(ends <= position, ends, 0.0), axis=0, keepdims=True)
    first = jnp.min(start).astype(jnp.int32)
    reach = jnp.maximum(index * ROWS - first + ROWS - 1, 0) // ROWS
    start = start.astype(jnp.int32)
    q_pos = lax.broadcasted_iota(jnp.int32, (1, 128), 1) + index * ROWS
    top[...] = jnp.full_like(top, NEG)
    total[...] = jnp.zeros_like(total)
    ot[...] = jnp.zeros_like(ot)
    dqt[...] = jnp.zeros_like(dqt)

    def live(plane):
        return jnp.maximum(4 * plane + y_place - 3, 0) <= reach

    pairs = [slice(256 * p, 256 * (p + 1)) for p in range(4)]

    def keys(plane, which):
        return kv_ref[:, plane, which].reshape(512, HEAD)

    def scores(plane, _):
        @pl.when(live(plane))
        def _():
            for y in range(4):
                back = (4 * plane + y_place - y) & 15
                k_pos = lax.broadcasted_iota(jnp.int32, (128, 128), 0) + (index - back) * ROWS
                bias[y * 128 : (y + 1) * 128, :] = jnp.where(
                    (k_pos >= start) & (k_pos <= q_pos), 0.0, NEG
                )
            key_quad = keys(plane, 0)
            for cols in pairs:
                raw = nn(key_quad, qt[:, cols])
                wide_bias = jnp.concatenate([bias[...], bias[...]], axis=1)
                raw = raw * (SCALE * LOG2E) + wide_bias
                s_ref[plane, :, cols] = raw
                top[:, cols] = jnp.maximum(top[:, cols], jnp.max(raw, axis=0, keepdims=True))

        return 0

    lax.fori_loop(0, 4, scores, 0)

    def weigh(plane, _):
        @pl.when(live(plane))
        def _():
            value_quad = keys(plane, 1)
            for cols in pairs:
                prob = jnp.exp2(s_ref[plane, :, cols] - top[:, cols])
                s_ref[plane, :, cols] = prob
                total[:, cols] += jnp.sum(prob, axis=0, keepdims=True)
                ot[:, cols] += tn(value_quad, prob.astype(BF16))

        return 0

    lax.fori_loop(0, 4, weigh, 0)
    total[...] = 1.0 / total[...]
    for n in range(GROUP):
        cols = slice(n * HEAD, (n + 1) * HEAD)
        o_n = (ot[:, cols] * total[:, cols]).astype(BF16)
        ot_ref[:, cols] = o_n
        delta[:, cols] = jnp.sum(
            o_n.astype(F32) * gt[:, cols].astype(F32), axis=0, keepdims=True
        )

    def grads(plane, _):
        @pl.when(live(plane))
        def _():
            key_quad = keys(plane, 0)
            value_quad = keys(plane, 1)
            for p, cols in enumerate(pairs):
                prob = s_ref[plane, :, cols] * total[:, cols]
                grad_prob = nn(value_quad, gt[:, cols])
                grad_score = (prob * (grad_prob - delta[:, cols])).astype(BF16)
                dqt[:, cols] += tn(key_quad, grad_score)
                part_k = nn(grad_score, qs[cols, :])
                part_v = nn(prob.astype(BF16), gs[cols, :])
                if p == 0:
                    dk[...] = part_k
                    dv[...] = part_v
                else:
                    dk[...] += part_k
                    dv[...] += part_v
            dkv_ref[:, plane, 0] = (dk[...] * SCALE).astype(BF16).reshape(4, 128, HEAD)
            dkv_ref[:, plane, 1] = dv[...].astype(BF16).reshape(4, 128, HEAD)

        @pl.when(jnp.logical_not(live(plane)))
        def _():
            for y in range(4):
                dkv_ref[y, plane] = jnp.zeros((2, 128, HEAD), BF16)

        return 0

    lax.fori_loop(0, 4, grads, 0)
    dqt_ref[...] = (dqt[...] * SCALE).astype(BF16)


def finish_kernel(dqt_ref, ot_ref, low_ref, od_ref, qu_ref, dq_ref, back_ref, tot_ref):
    xa_q = low_ref[0:16]
    u = low_ref[48:64]
    out_adapter = jnp.zeros((RANK, ROWS), F32)
    back_q = jnp.zeros((RANK, ROWS), F32)
    for n in range(GROUP):
        cols = slice(n * HEAD, (n + 1) * HEAD)
        dq_t = dqt_ref[:, cols]
        dq_n = dq_t.T
        dq_ref[:, cols] = dq_n
        back_q = back_q + nn(qu_ref[:, cols], dq_t)
        tot_ref[GROUP + n] = (ADAPTER_SCALE * nn(xa_q, dq_n)).astype(BF16)
        o_n = ot_ref[:, cols]
        out_adapter = out_adapter + nn(od_ref[:, cols], o_n)
        tot_ref[n] = (ADAPTER_SCALE * nt(u, o_n)).astype(BF16)
    back_ref[0:16] = out_adapter.astype(BF16)
    back_ref[16:32] = back_q.astype(BF16)


def gather_kernel(y_ref, back_ref, ku_ref, vu_ref, part_ref, out_ref):
    y = lax.axis_index("ctx") % 4
    parts = []
    for plane in range(5):
        term = [y_ref[source, plane % 4].astype(F32) for source in range(4)]
        if plane == 0:
            term = [term[source] * (source >= y).astype(F32) for source in range(4)]
        if plane == 4:
            term = [term[source] * (source < y).astype(F32) for source in range(4)]
        acc = (term[0] + term[1] + term[2] + term[3]).astype(BF16)
        part_ref[plane] = acc
        parts += [nt(ku_ref[...], acc[0]), nt(vu_ref[...], acc[1])]
    parts = jnp.concatenate(parts, axis=0).astype(BF16)
    for peer in range(8):
        out_ref[peer, 0:32] = back_ref[...]
        out_ref[peer, 32:192] = parts


def down_kernel(
    low_ref, x_ref, one_ref, two_ref, four_ref, dout_ref, part_ref, sum_ref, tot_ref, out_ref
):
    low = low_ref[0].astype(F32)
    for peer in range(1, 8):
        low = low + low_ref[peer].astype(F32)
    low = low.astype(BF16)
    near = nn(low[16:64], x_ref[...])
    fars = (one_ref[...], two_ref[0], two_ref[1], four_ref[...])
    tiles = [near[0:16, t * 128 : (t + 1) * 128] for t in range(5)]
    down = []
    for t in range(5):
        acc = near[16:48, t * 128 : (t + 1) * 128]
        for p, far in enumerate(fars):
            acc = acc + nn(low[64 + 32 * p : 96 + 32 * p], far[t * 128 : (t + 1) * 128])
        down.append(acc)
    tiles += [acc[0:16] for acc in down] + [acc[16:32] for acc in down]
    up = nn(low[0:16], dout_ref[...])
    tiles += [up[:, t * 128 : (t + 1) * 128] for t in range(5)]
    tiles = [(ADAPTER_SCALE * tile).astype(BF16) for tile in tiles]
    tiles += [tot_ref[t] for t in range(16)]
    for which in range(2):
        rows = slice(16 * which, 16 * which + 16)
        acc = nn(sum_ref[16 + 16 * which : 32 + 16 * which], part_ref[0, which])
        for p, far in enumerate(fars):
            acc = acc + nn(far[640:672][rows], part_ref[p + 1, which])
        tiles.append((ADAPTER_SCALE * acc).astype(BF16))
    zero = jnp.zeros((16, 128), BF16)
    tiles += [zero, zero]
    for t, tile in enumerate(tiles):
        out_ref[t // 5, t % 5] = tile


def pass_two_kernel(part_ref, four_ref, out_ref):
    out_ref[0] = part_ref[2]
    out_ref[1] = (part_ref[3].astype(F32) + four_ref[...].astype(F32)).astype(BF16)


def pass_kernel(part_ref, two_ref, out_ref):
    out_ref[...] = (part_ref[1].astype(F32) + two_ref[1].astype(F32)).astype(BF16)


def owner_kernel(part_ref, one_ref, two_ref, dk_ref, dv_ref):
    for which, ref in enumerate((dk_ref, dv_ref)):
        acc = part_ref[0, which].astype(F32) + one_ref[which].astype(F32)
        ref[...] = (acc + two_ref[0, which].astype(F32)).astype(BF16)


def sum_spread_kernel(in_ref, out_ref):
    acc = in_ref[0].astype(F32)
    for peer in range(1, 8):
        acc = acc + in_ref[peer].astype(F32)
    acc = acc.astype(BF16)
    for peer in range(8):
        out_ref[peer] = acc


def unpack_kernel(in_ref, qd_ref, qu_ref, kd_ref, ku_ref, vd_ref, vu_ref, od_ref, ou_ref):
    def tile(t):
        return in_ref[t // 5, t % 5].astype(F32)

    for which, ref in enumerate((qd_ref, kd_ref, vd_ref, ou_ref)):
        for t in range(5):
            ref[:, t * 128 : (t + 1) * 128] = tile(which * 5 + t)
    for t in range(8):
        od_ref[:, t * 128 : (t + 1) * 128] = tile(20 + t)
        qu_ref[:, t * 128 : (t + 1) * 128] = tile(28 + t)
    ku_ref[...] = tile(36)
    vu_ref[...] = tile(37)


def shift(value, steps):
    count = lax.axis_size("ctx")
    first, last = max(0, -steps), min(count, count - steps)
    return lax.ppermute(value, "ctx", [(i, i + steps) for i in range(first, last)])


def exchange(value, groups):
    return lax.all_to_all(value, "ctx", 0, 0, tiled=True, axis_index_groups=groups)


def exchange_head(value):
    return lax.all_to_all(value, "head", 0, 0, tiled=True)


def after(value, *others):
    return lax.optimization_barrier((value, *others))[0]


def shards(x, q, keys, values, frozen, dout, lengths, qd, qu, kd, ku, vd, vu, od, ou):
    qd, kd, vd, od = qd.T, kd.T, vd.T, od.T
    wide = shaped((128, 1024), BF16)
    tall = shaped((1024, 128), BF16)
    block = shaped((2, 128, 128), BF16)
    pair = jnp.stack([keys, values])
    four = shift(pair, 16)
    one = shift(pair, 4)
    low = call(project_kernel, shaped((8, 64, 128), BF16), x, dout, qd, kd, vd, ou, vmem=60)
    low = exchange_head(after(low, one))
    two = shift(jnp.stack([pair, one]), 8)
    window, x_rows, low = call(
        spread_kernel,
        (shaped((4, 4, 2, 128, 128), BF16), shaped((672, 128), BF16), shaped((64, 128), BF16)),
        pair, one, two, four, low, x,
    )
    window = exchange(window, Y_GROUPS)
    x_one = shift(x_rows, 4)
    qs, qt, gs, gt = call(prepare_kernel, (tall, wide, tall, wide), q, frozen, low, od)
    x_two = shift(jnp.stack([x_rows, x_one]), 8)
    x_four = shift(x_two[1], 4)
    dqt, ot, dkv = call(
        attention_kernel,
        (wide, wide, shaped((4, 4, 2, 128, 128), BF16)),
        after(qs, x_one), qt, gs, gt, window, lengths.reshape(1, 128),
        scratch=[
            pltpu.VMEM((4, 512, 1024), F32),
            pltpu.VMEM((128, 1024), F32),
            pltpu.VMEM((128, 1024), F32),
            pltpu.VMEM((512, 128), F32),
            pltpu.VMEM((512, 128), F32),
            pltpu.VMEM((512, 128), F32),
            pltpu.VMEM((1, 1024), F32),
            pltpu.VMEM((1, 1024), F32),
            pltpu.VMEM((1, 1024), F32),
        ],
        vmem=24,
        flops=3 << 30,
    )
    dkv = exchange(after(dkv, x_two), Y_GROUPS)
    dq, back, totals = call(
        finish_kernel,
        (wide, shaped((32, 128), BF16), shaped((16, 16, 128), BF16)),
        dqt, ot, low, od, qu,
    )
    parts, low_back = call(
        gather_kernel,
        (shaped((5, 2, 128, 128), BF16), shaped((8, 192, 128), BF16)),
        dkv, back, ku, vu,
    )
    four_back = shift(parts[4], -4)
    low_back = exchange_head(after(low_back, x_four))
    packed = shaped((8, 5, 16, 128), BF16)
    sums = call(
        down_kernel, packed, low_back, x, x_one, x_two, x_four, dout, parts, low, totals
    )
    sums = after(exchange(sums, EIGHTS), four_back)
    sums = call(sum_spread_kernel, packed, sums)
    two_back = shift(call(pass_two_kernel, shaped((2, 2, 128, 128), BF16), parts, four_back), -8)
    sums = after(exchange(sums, STRIDED), two_back)
    sums = call(sum_spread_kernel, packed, sums)
    sums = exchange(sums, EIGHTS)
    one_back = shift(call(pass_kernel, block, parts, two_back), -4)
    dk, dv = call(
        owner_kernel,
        (shaped((128, 128), BF16), shaped((128, 128), BF16)),
        parts, one_back, two_back,
    )
    narrow, small = shaped((16, 640), F32), shaped((16, 128), F32)
    broad = shaped((16, 1024), F32)
    g_qd, g_qu, g_kd, g_ku, g_vd, g_vu, g_od, g_ou = call(
        unpack_kernel, (narrow, broad, narrow, small, narrow, small, broad, narrow), sums
    )
    return dq, dk, dv, g_qd.T, g_qu, g_kd.T, g_ku, g_vd.T, g_vu, g_od.T, g_ou


def solution(mesh):
    rows, cols, tokens = P("head", None), P(None, "head"), P("ctx", "head")
    return jax.shard_map(
        shards,
        mesh=mesh,
        in_specs=(tokens,) * 6 + (P(),) + (rows, cols) * 4,
        out_specs=(tokens,) * 3 + (rows, cols) * 4,
        check_vma=False,
    )
```

```python
import functools

import jax
import jax.numpy as jnp
from jax import lax
from jax.experimental import pallas as pl
from jax.experimental.pallas import tpu as pltpu
from jax.sharding import PartitionSpec as P

HEAD = 128
ROWS = 128
GROUP = 8
RANK = 16
TILES = 40
SCALE = HEAD**-0.5
LOG2E = 1.4426950408889634
ADAPTER_SCALE = 2.0
NEG = -1e30
F32 = jnp.float32
BF16 = jnp.bfloat16

Y_GROUPS = [[4 * z + y for y in range(4)] for z in range(16)]
EIGHTS = [[8 * g + i for i in range(8)] for g in range(8)]
STRIDED = [[g + 8 * i for i in range(8)] for g in range(8)]


def nn(a, b):
    return lax.dot_general(a, b, (((1,), (0,)), ((), ())), preferred_element_type=F32)


def nt(a, b):
    return lax.dot_general(a, b, (((1,), (1,)), ((), ())), preferred_element_type=F32)


def tn(a, b):
    return lax.dot_general(a, b, (((0,), (0,)), ((), ())), preferred_element_type=F32)


def call(body, outs, *args, scratch=(), vmem=32, flops=1 << 20):
    return pl.pallas_call(
        body,
        out_shape=outs,
        scratch_shapes=list(scratch),
        compiler_params=pltpu.CompilerParams(vmem_limit_bytes=vmem << 20),
        cost_estimate=pl.CostEstimate(flops=flops, bytes_accessed=1 << 20, transcendentals=0),
    )(*args)


def shaped(shape, dtype):
    return jax.ShapeDtypeStruct(shape, dtype)


def project_kernel(x_ref, dout_ref, qd_ref, kd_ref, vd_ref, ou_ref, out_ref):
    parts = [nt(ref[...], x_ref[...]) for ref in (qd_ref, kd_ref, vd_ref)]
    parts.append(nt(ou_ref[...], dout_ref[...]))
    low = jnp.concatenate(parts, axis=0).astype(BF16)
    for peer in range(8):
        out_ref[peer] = low


def spread_kernel(
    pair_ref, one_ref, two_ref, back_ref, low_ref, x_ref, out_ref, x_out, sum_ref
):
    y = lax.axis_index("ctx") % 4
    for dest in range(4):

        @pl.when(dest >= y)
        def _(dest=dest):
            out_ref[dest, 0] = pair_ref[...]

        @pl.when(dest < y)
        def _(dest=dest):
            out_ref[dest, 0] = back_ref[1]

        out_ref[dest, 1] = one_ref[...]
        out_ref[dest, 2] = two_ref[...]
        out_ref[dest, 3] = back_ref[0]
    low = low_ref[0].astype(F32)
    for peer in range(1, 8):
        low = low + low_ref[peer].astype(F32)
    low = low.astype(BF16)
    sum_ref[...] = low
    for t in range(5):
        x_out[t * 128 : (t + 1) * 128, :] = x_ref[:, t * 128 : (t + 1) * 128]
    x_out[640:672, :] = low[16:48]


def prepare_kernel(
    q_ref, f_ref, low_ref, od_ref, len_ref, qs_ref, qt_ref, gs_ref, gt_ref, start_ref
):
    doc = lax.broadcasted_iota(jnp.int32, (128, 128), 0)
    lane = lax.broadcasted_iota(jnp.int32, (128, 128), 1)
    lengths = jnp.broadcast_to(len_ref[...].astype(F32), (128, 128))
    ends = jnp.sum(jnp.where(lane <= doc, lengths, 0.0), axis=1, keepdims=True)
    position = (lane + lax.axis_index("ctx") * ROWS).astype(F32)
    start = jnp.max(jnp.where(ends <= position, ends, 0.0), axis=0, keepdims=True)
    start_ref[...] = jnp.broadcast_to(start, (8, 128))
    u = low_ref[48:64]
    for n in range(GROUP):
        cols = slice(n * HEAD, (n + 1) * HEAD)
        q_n = q_ref[:, cols]
        qs_ref[cols, :] = q_n
        qt_ref[:, cols] = q_n.T
        g_n = f_ref[:, cols].astype(F32) + ADAPTER_SCALE * tn(u, od_ref[:, cols])
        g_n = g_n.astype(BF16)
        gs_ref[cols, :] = g_n
        gt_ref[:, cols] = g_n.T


def attention_kernel(
    qs, qt, gs, gt, kv_ref, start_ref,
    dqt_ref, ot_ref, dkv_ref,
    s_ref, ot, dqt, ds, low_prob, bias, top, total, delta,
):
    index = lax.axis_index("ctx")
    y_place = index % 4
    start = start_ref[0:1]
    start = start.astype(jnp.int32)
    q_pos = lax.broadcasted_iota(jnp.int32, (1, 128), 1) + index * ROWS
    top[...] = jnp.full_like(top, NEG)
    total[...] = jnp.zeros_like(total)
    ot[...] = jnp.zeros_like(ot)
    dqt[...] = jnp.zeros_like(dqt)

    def keys(plane, which):
        return kv_ref[:, plane, which].reshape(512, HEAD)

    for plane in range(4):
        for y in range(4):
            back = (4 * plane + y_place - y) & 15
            k_pos = lax.broadcasted_iota(jnp.int32, (128, 128), 0) + (index - back) * ROWS
            bias[y * 128 : (y + 1) * 128, :] = jnp.where(
                (k_pos >= start) & (k_pos <= q_pos), 0.0, NEG
            )
        raw = nn(keys(plane, 0), qt[...])
        raw = raw * (SCALE * LOG2E) + jnp.concatenate([bias[...]] * GROUP, axis=1)
        s_ref[plane] = raw
        top[...] = jnp.maximum(top[...], jnp.max(raw, axis=0, keepdims=True))
    for plane in range(4):
        prob = jnp.exp2(s_ref[plane] - top[...])
        s_ref[plane] = prob
        total[...] += jnp.sum(prob, axis=0, keepdims=True)
        ot[...] += nn(keys(plane, 1).T, prob.astype(BF16))
    total[...] = 1.0 / total[...]
    for n in range(GROUP):
        cols = slice(n * HEAD, (n + 1) * HEAD)
        o_n = (ot[:, cols] * total[:, cols]).astype(BF16)
        ot_ref[:, cols] = o_n
        delta[:, cols] = jnp.sum(
            o_n.astype(F32) * gt[:, cols].astype(F32), axis=0, keepdims=True
        )
    for plane in range(4):
        prob = s_ref[plane] * total[...]
        grad_prob = nn(keys(plane, 1), gt[...])
        grad_score = (prob * (grad_prob - delta[...])).astype(BF16)
        ds[...] = grad_score
        low_prob[...] = prob.astype(BF16)
        dqt[...] += nn(keys(plane, 0).T, grad_score)
        dk = (nn(ds[...], qs[...]) * SCALE).astype(BF16)
        dv = nn(low_prob[...], gs[...]).astype(BF16)
        dkv_ref[:, plane, 0] = dk.reshape(4, 128, HEAD)
        dkv_ref[:, plane, 1] = dv.reshape(4, 128, HEAD)
    dqt_ref[...] = (dqt[...] * SCALE).astype(BF16)


def finish_kernel(dqt_ref, ot_ref, low_ref, od_ref, qu_ref, dq_ref, back_ref, tot_ref):
    xa_q = low_ref[0:16]
    u = low_ref[48:64]
    out_adapter = jnp.zeros((RANK, ROWS), F32)
    back_q = jnp.zeros((RANK, ROWS), F32)
    for n in range(GROUP):
        cols = slice(n * HEAD, (n + 1) * HEAD)
        dq_t = dqt_ref[:, cols]
        dq_n = dq_t.T
        dq_ref[:, cols] = dq_n
        back_q = back_q + nn(qu_ref[:, cols], dq_t)
        tot_ref[GROUP + n] = (ADAPTER_SCALE * nn(xa_q, dq_n)).astype(BF16)
        o_n = ot_ref[:, cols]
        out_adapter = out_adapter + nn(od_ref[:, cols], o_n)
        tot_ref[n] = (ADAPTER_SCALE * nt(u, o_n)).astype(BF16)
    back_ref[0:16] = out_adapter.astype(BF16)
    back_ref[16:32] = back_q.astype(BF16)


def gather_kernel(y_ref, back_ref, ku_ref, vu_ref, part_ref, send_ref, out_ref):
    y = lax.axis_index("ctx") % 4
    parts = []
    for plane in range(5):
        term = [y_ref[source, plane % 4].astype(F32) for source in range(4)]
        if plane == 0:
            term = [term[source] * (source >= y).astype(F32) for source in range(4)]
        if plane == 4:
            term = [term[source] * (source < y).astype(F32) for source in range(4)]
        acc = (term[0] + term[1] + term[2] + term[3]).astype(BF16)
        part_ref[plane] = acc
        if plane in (2, 4):
            send_ref[plane // 2 - 1] = acc
        parts += [nt(ku_ref[...], acc[0]), nt(vu_ref[...], acc[1])]
    parts = jnp.concatenate(parts, axis=0).astype(BF16)
    for peer in range(8):
        out_ref[peer, 0:32] = back_ref[...]
        out_ref[peer, 32:192] = parts


def down_kernel(
    low_ref, x_ref, one_ref, two_ref, three_ref, four_ref, dout_ref, part_ref, sum_ref, tot_ref, out_ref
):
    low = low_ref[0].astype(F32)
    for peer in range(1, 8):
        low = low + low_ref[peer].astype(F32)
    low = low.astype(BF16)
    near = nn(low[16:64], x_ref[...])
    fars = (one_ref, two_ref, three_ref, four_ref)
    tiles = [near[0:16, t * 128 : (t + 1) * 128] for t in range(5)]
    down = []
    for t in range(5):
        acc = near[16:48, t * 128 : (t + 1) * 128]
        for p, far in enumerate(fars):
            acc = acc + nn(low[64 + 32 * p : 96 + 32 * p], far[t * 128 : (t + 1) * 128])
        down.append(acc)
    tiles += [acc[0:16] for acc in down] + [acc[16:32] for acc in down]
    up = nn(low[0:16], dout_ref[...])
    tiles += [up[:, t * 128 : (t + 1) * 128] for t in range(5)]
    tiles = [(ADAPTER_SCALE * tile).astype(BF16) for tile in tiles]
    tiles += [tot_ref[t] for t in range(16)]
    for which in range(2):
        rows = slice(16 * which, 16 * which + 16)
        acc = nn(sum_ref[16 + 16 * which : 32 + 16 * which], part_ref[0, which])
        for p, far in enumerate(fars):
            acc = acc + nn(far[640 + rows.start : 640 + rows.stop], part_ref[p + 1, which])
        tiles.append((ADAPTER_SCALE * acc).astype(BF16))
    zero = jnp.zeros((16, 128), BF16)
    tiles += [zero, zero]
    for t, tile in enumerate(tiles):
        out_ref[t // 5, t % 5] = tile


def pass_kernel(part_ref, near_ref, one_ref, three_ref):
    one_ref[...] = (part_ref[1].astype(F32) + near_ref[0].astype(F32)).astype(BF16)
    three_ref[...] = (part_ref[3].astype(F32) + near_ref[1].astype(F32)).astype(BF16)


def owner_kernel(part_ref, one_ref, three_ref, dk_ref, dv_ref):
    for which, ref in enumerate((dk_ref, dv_ref)):
        acc = part_ref[0, which].astype(F32) + one_ref[which].astype(F32)
        ref[...] = (acc + three_ref[which].astype(F32)).astype(BF16)


def sum_spread_kernel(in_ref, out_ref):
    acc = in_ref[0].astype(F32)
    for peer in range(1, 8):
        acc = acc + in_ref[peer].astype(F32)
    acc = acc.astype(BF16)
    for peer in range(8):
        out_ref[peer] = acc


def unpack_kernel(in_ref, qd_ref, qu_ref, kd_ref, ku_ref, vd_ref, vu_ref, od_ref, ou_ref):
    def tile(t):
        return in_ref[t // 5, t % 5].astype(F32)

    for which, ref in enumerate((qd_ref, kd_ref, vd_ref, ou_ref)):
        for t in range(5):
            ref[:, t * 128 : (t + 1) * 128] = tile(which * 5 + t)
    for t in range(8):
        od_ref[:, t * 128 : (t + 1) * 128] = tile(20 + t)
        qu_ref[:, t * 128 : (t + 1) * 128] = tile(28 + t)
    ku_ref[...] = tile(36)
    vu_ref[...] = tile(37)


def shift(value, steps):
    count = lax.axis_size("ctx")
    first, last = max(0, -steps), min(count, count - steps)
    return lax.ppermute(value, "ctx", [(i, i + steps) for i in range(first, last)])


def exchange(value, groups):
    return lax.all_to_all(value, "ctx", 0, 0, tiled=True, axis_index_groups=groups)


def exchange_head(value):
    return lax.all_to_all(value, "head", 0, 0, tiled=True)


def after(value, *others):
    return lax.optimization_barrier((value, *others))[0]


def shards(x, q, keys, values, frozen, dout, lengths, qd, qu, kd, ku, vd, vu, od, ou):
    qd, kd, vd, od = qd.T, kd.T, vd.T, od.T
    wide = shaped((128, 1024), BF16)
    tall = shaped((1024, 128), BF16)
    block = shaped((2, 128, 128), BF16)
    pair = jnp.stack([keys, values])
    one = shift(pair, 4)
    low = call(project_kernel, shaped((8, 64, 128), BF16), x, dout, qd, kd, vd, ou)
    low = exchange_head(after(low, one))
    two, back = shift(one, 4), shift(jnp.stack([pair, one]), 12)
    window, x_rows, low = call(
        spread_kernel,
        (shaped((4, 4, 2, 128, 128), BF16), shaped((672, 128), BF16), shaped((64, 128), BF16)),
        pair, one, two, back, low, x,
    )
    window = exchange(window, Y_GROUPS)
    x_one = shift(x_rows, 4)
    x_two = shift(x_rows, 8)
    x_three, x_four = shift(x_two, 4), shift(x_two, 8)
    qs, qt, gs, gt, starts = call(
        prepare_kernel,
        (tall, wide, tall, wide, shaped((8, 128), F32)),
        q, frozen, low, od, lengths.reshape(1, 128),
    )
    dqt, ot, dkv = call(
        attention_kernel,
        (wide, wide, shaped((4, 4, 2, 128, 128), BF16)),
        qs, qt, gs, gt, window, starts,
        scratch=[
            pltpu.VMEM((4, 512, 1024), F32),
            pltpu.VMEM((128, 1024), F32),
            pltpu.VMEM((128, 1024), F32),
            pltpu.VMEM((512, 1024), BF16),
            pltpu.VMEM((512, 1024), BF16),
            pltpu.VMEM((512, 128), F32),
            pltpu.VMEM((1, 1024), F32),
            pltpu.VMEM((1, 1024), F32),
            pltpu.VMEM((1, 1024), F32),
        ],
        vmem=40,
        flops=3 << 30,
    )
    dkv = exchange(after(dkv, x_one, x_two), Y_GROUPS)
    dq, back, totals = call(
        finish_kernel,
        (wide, shaped((32, 128), BF16), shaped((16, 16, 128), BF16)),
        dqt, ot, low, od, qu,
    )
    parts, near, low_back = call(
        gather_kernel,
        (
            shaped((5, 2, 128, 128), BF16),
            shaped((2, 2, 128, 128), BF16),
            shaped((8, 192, 128), BF16),
        ),
        dkv, back, ku, vu,
    )
    near = shift(near, -4)
    low_back = exchange_head(after(low_back, x_three, x_four))
    low_back = after(low_back, near)
    packed = shaped((8, 5, 16, 128), BF16)
    sums = call(
        down_kernel, packed, low_back, x, x_one, x_two, x_three, x_four, dout, parts, low, totals
    )
    sums = call(sum_spread_kernel, packed, exchange(sums, EIGHTS))
    one_back, three_back = call(pass_kernel, (block, block), parts, near)
    one_back, three_back = shift(one_back, -4), shift(three_back, -12)
    sums = after(exchange(sums, STRIDED), one_back, three_back)
    sums = call(sum_spread_kernel, packed, sums)
    sums = exchange(sums, EIGHTS)
    dk, dv = call(
        owner_kernel,
        (shaped((128, 128), BF16), shaped((128, 128), BF16)),
        parts, one_back, three_back,
    )
    narrow, small = shaped((16, 640), F32), shaped((16, 128), F32)
    broad = shaped((16, 1024), F32)
    g_qd, g_qu, g_kd, g_ku, g_vd, g_vu, g_od, g_ou = call(
        unpack_kernel, (narrow, broad, narrow, small, narrow, small, broad, narrow), sums
    )
    return dq, dk, dv, g_qd.T, g_qu, g_kd.T, g_ku, g_vd.T, g_vu, g_od.T, g_ou


def solution(mesh):
    rows, cols, tokens = P("head", None), P(None, "head"), P("ctx", "head")
    return jax.shard_map(
        shards,
        mesh=mesh,
        in_specs=(tokens,) * 6 + (P(),) + (rows, cols) * 4,
        out_specs=(tokens,) * 3 + (rows, cols) * 4,
        check_vma=False,
    )
```

```python
import functools

import jax
import jax.numpy as jnp
from jax import lax
from jax.experimental import pallas as pl
from jax.experimental.pallas import tpu as pltpu
from jax.sharding import PartitionSpec as P

HEAD = 128
ROWS = 128
GROUP = 8
RANK = 16
TILES = 40
SCALE = HEAD**-0.5
LOG2E = 1.4426950408889634
ADAPTER_SCALE = 2.0
NEG = -1e30
F32 = jnp.float32
BF16 = jnp.bfloat16

Y_GROUPS = [[4 * z + y for y in range(4)] for z in range(16)]
EIGHTS = [[8 * g + i for i in range(8)] for g in range(8)]
STRIDED = [[g + 8 * i for i in range(8)] for g in range(8)]


def nn(a, b):
    return lax.dot_general(a, b, (((1,), (0,)), ((), ())), preferred_element_type=F32)


def nt(a, b):
    return lax.dot_general(a, b, (((1,), (1,)), ((), ())), preferred_element_type=F32)


def tn(a, b):
    return lax.dot_general(a, b, (((0,), (0,)), ((), ())), preferred_element_type=F32)


def call(body, outs, *args, scratch=(), vmem=32, flops=1 << 20):
    return pl.pallas_call(
        body,
        out_shape=outs,
        scratch_shapes=list(scratch),
        compiler_params=pltpu.CompilerParams(vmem_limit_bytes=vmem << 20),
        cost_estimate=pl.CostEstimate(flops=flops, bytes_accessed=1 << 20, transcendentals=0),
    )(*args)


def shaped(shape, dtype):
    return jax.ShapeDtypeStruct(shape, dtype)


def project_kernel(x_ref, dout_ref, qd_ref, kd_ref, vd_ref, ou_ref, out_ref):
    parts = [nt(ref[...], x_ref[...]) for ref in (qd_ref, kd_ref, vd_ref)]
    parts.append(nt(ou_ref[...], dout_ref[...]))
    low = jnp.concatenate(parts, axis=0).astype(BF16)
    for peer in range(8):
        out_ref[peer] = low


def spread_kernel(
    pair_ref, one_ref, two_ref, back_ref, low_ref, x_ref, out_ref, x_out, sum_ref
):
    y = lax.axis_index("ctx") % 4
    for dest in range(4):

        @pl.when(dest >= y)
        def _(dest=dest):
            out_ref[dest, 0] = pair_ref[...]

        @pl.when(dest < y)
        def _(dest=dest):
            out_ref[dest, 0] = back_ref[1]

        out_ref[dest, 1] = one_ref[...]
        out_ref[dest, 2] = two_ref[...]
        out_ref[dest, 3] = back_ref[0]
    low = low_ref[0].astype(F32)
    for peer in range(1, 8):
        low = low + low_ref[peer].astype(F32)
    low = low.astype(BF16)
    sum_ref[...] = low
    for t in range(5):
        x_out[t * 128 : (t + 1) * 128, :] = x_ref[:, t * 128 : (t + 1) * 128]
    x_out[640:672, :] = low[16:48]


def prepare_kernel(
    q_ref, f_ref, low_ref, od_ref, len_ref, qs_ref, qt_ref, gs_ref, gt_ref, start_ref
):
    doc = lax.broadcasted_iota(jnp.int32, (128, 128), 0)
    lane = lax.broadcasted_iota(jnp.int32, (128, 128), 1)
    lengths = jnp.broadcast_to(len_ref[...].astype(F32), (128, 128))
    ends = jnp.sum(jnp.where(lane <= doc, lengths, 0.0), axis=1, keepdims=True)
    position = (lane + lax.axis_index("ctx") * ROWS).astype(F32)
    start = jnp.max(jnp.where(ends <= position, ends, 0.0), axis=0, keepdims=True)
    start_ref[...] = jnp.broadcast_to(start, (8, 128))
    u = low_ref[48:64]
    for n in range(GROUP):
        cols = slice(n * HEAD, (n + 1) * HEAD)
        q_n = q_ref[:, cols]
        qs_ref[cols, :] = q_n
        qt_ref[:, cols] = q_n.T
        g_n = f_ref[:, cols].astype(F32) + ADAPTER_SCALE * tn(u, od_ref[:, cols])
        g_n = g_n.astype(BF16)
        gs_ref[cols, :] = g_n
        gt_ref[:, cols] = g_n.T


def attention_kernel(
    qs, qt, gs, gt, kv_ref, start_ref,
    dqt_ref, ot_ref, dkv_ref,
    s_ref, wide_low, bias, total, delta,
):
    index = lax.axis_index("ctx")
    y_place = index % 4
    start = start_ref[0:1]
    start = start.astype(jnp.int32)
    q_pos = lax.broadcasted_iota(jnp.int32, (1, 128), 1) + index * ROWS

    def keys(plane, which):
        return kv_ref[:, plane, which].reshape(512, HEAD)

    for plane in range(4):
        for y in range(4):
            back = (4 * plane + y_place - y) & 15
            k_pos = lax.broadcasted_iota(jnp.int32, (128, 128), 0) + (index - back) * ROWS
            bias[y * 128 : (y + 1) * 128, :] = jnp.where(
                (k_pos >= start) & (k_pos <= q_pos), 0.0, NEG
            )
        raw = nn(keys(plane, 0), qt[...])
        raw = raw * (SCALE * LOG2E) + jnp.concatenate([bias[...]] * GROUP, axis=1)
        s_ref[plane] = raw
        best = jnp.max(raw, axis=0, keepdims=True)
        peak = best if plane == 0 else jnp.maximum(peak, best)
    values_t = jnp.concatenate([keys(plane, 1).T for plane in range(4)], axis=1)
    norm = jnp.zeros((1, 1024), F32)
    for plane in range(4):
        prob = jnp.exp2(s_ref[plane] - peak)
        s_ref[plane] = prob
        norm = norm + jnp.sum(prob, axis=0, keepdims=True)
        wide_low[plane * 512 : plane * 512 + 512, :] = prob.astype(BF16)
    weighted = nn(values_t, wide_low[...])
    total[...] = 1.0 / norm
    for n in range(GROUP):
        cols = slice(n * HEAD, (n + 1) * HEAD)
        o_n = (weighted[:, cols] * total[:, cols]).astype(BF16)
        ot_ref[:, cols] = o_n
        delta[:, cols] = jnp.sum(
            o_n.astype(F32) * gt[:, cols].astype(F32), axis=0, keepdims=True
        )
    for plane in range(4):
        prob = s_ref[plane] * total[...]
        grad_prob = nn(keys(plane, 1), gt[...])
        grad_score = (prob * (grad_prob - delta[...])).astype(BF16)
        wide_low[plane * 512 : plane * 512 + 512, :] = grad_score
        dk = (nn(grad_score, qs[...]) * SCALE).astype(BF16)
        dv = nn(prob.astype(BF16), gs[...]).astype(BF16)
        dkv_ref[:, plane, 0] = dk.reshape(4, 128, HEAD)
        dkv_ref[:, plane, 1] = dv.reshape(4, 128, HEAD)
    keys_t = jnp.concatenate([keys(plane, 0).T for plane in range(4)], axis=1)
    dqt_ref[...] = (nn(keys_t, wide_low[...]) * SCALE).astype(BF16)


def finish_kernel(dqt_ref, ot_ref, low_ref, od_ref, qu_ref, dq_ref, back_ref, tot_ref):
    xa_q = low_ref[0:16]
    u = low_ref[48:64]
    out_adapter = jnp.zeros((RANK, ROWS), F32)
    back_q = jnp.zeros((RANK, ROWS), F32)
    for n in range(GROUP):
        cols = slice(n * HEAD, (n + 1) * HEAD)
        dq_t = dqt_ref[:, cols]
        dq_n = dq_t.T
        dq_ref[:, cols] = dq_n
        back_q = back_q + nn(qu_ref[:, cols], dq_t)
        tot_ref[GROUP + n] = (ADAPTER_SCALE * nn(xa_q, dq_n)).astype(BF16)
        o_n = ot_ref[:, cols]
        out_adapter = out_adapter + nn(od_ref[:, cols], o_n)
        tot_ref[n] = (ADAPTER_SCALE * nt(u, o_n)).astype(BF16)
    back_ref[0:16] = out_adapter.astype(BF16)
    back_ref[16:32] = back_q.astype(BF16)


def gather_kernel(y_ref, back_ref, ku_ref, vu_ref, part_ref, send_ref, out_ref):
    y = lax.axis_index("ctx") % 4
    parts = []
    for plane in range(5):
        term = [y_ref[source, plane % 4].astype(F32) for source in range(4)]
        if plane == 0:
            term = [term[source] * (source >= y).astype(F32) for source in range(4)]
        if plane == 4:
            term = [term[source] * (source < y).astype(F32) for source in range(4)]
        acc = (term[0] + term[1] + term[2] + term[3]).astype(BF16)
        part_ref[plane] = acc
        if plane in (2, 4):
            send_ref[plane // 2 - 1] = acc
        parts += [nt(ku_ref[...], acc[0]), nt(vu_ref[...], acc[1])]
    parts = jnp.concatenate(parts, axis=0).astype(BF16)
    for peer in range(8):
        out_ref[peer, 0:32] = back_ref[...]
        out_ref[peer, 32:192] = parts


def down_kernel(
    low_ref, x_ref, one_ref, two_ref, three_ref, four_ref, dout_ref, part_ref, sum_ref, tot_ref, out_ref
):
    low = low_ref[0].astype(F32)
    for peer in range(1, 8):
        low = low + low_ref[peer].astype(F32)
    low = low.astype(BF16)
    near = nn(low[16:64], x_ref[...])
    fars = (one_ref, two_ref, three_ref, four_ref)
    tiles = [near[0:16, t * 128 : (t + 1) * 128] for t in range(5)]
    down = []
    for t in range(5):
        acc = near[16:48, t * 128 : (t + 1) * 128]
        for p, far in enumerate(fars):
            acc = acc + nn(low[64 + 32 * p : 96 + 32 * p], far[t * 128 : (t + 1) * 128])
        down.append(acc)
    tiles += [acc[0:16] for acc in down] + [acc[16:32] for acc in down]
    up = nn(low[0:16], dout_ref[...])
    tiles += [up[:, t * 128 : (t + 1) * 128] for t in range(5)]
    tiles = [(ADAPTER_SCALE * tile).astype(BF16) for tile in tiles]
    tiles += [tot_ref[t] for t in range(16)]
    for which in range(2):
        rows = slice(16 * which, 16 * which + 16)
        acc = nn(sum_ref[16 + 16 * which : 32 + 16 * which], part_ref[0, which])
        for p, far in enumerate(fars):
            acc = acc + nn(far[640 + rows.start : 640 + rows.stop], part_ref[p + 1, which])
        tiles.append((ADAPTER_SCALE * acc).astype(BF16))
    zero = jnp.zeros((16, 128), BF16)
    tiles += [zero, zero]
    for t, tile in enumerate(tiles):
        out_ref[t // 5, t % 5] = tile


def pass_kernel(part_ref, near_ref, one_ref, three_ref):
    one_ref[...] = (part_ref[1].astype(F32) + near_ref[0].astype(F32)).astype(BF16)
    three_ref[...] = (part_ref[3].astype(F32) + near_ref[1].astype(F32)).astype(BF16)


def owner_kernel(part_ref, one_ref, three_ref, dk_ref, dv_ref):
    for which, ref in enumerate((dk_ref, dv_ref)):
        acc = part_ref[0, which].astype(F32) + one_ref[which].astype(F32)
        ref[...] = (acc + three_ref[which].astype(F32)).astype(BF16)


def sum_spread_kernel(in_ref, out_ref):
    acc = in_ref[0].astype(F32)
    for peer in range(1, 8):
        acc = acc + in_ref[peer].astype(F32)
    acc = acc.astype(BF16)
    for peer in range(8):
        out_ref[peer] = acc


def unpack_kernel(in_ref, qd_ref, qu_ref, kd_ref, ku_ref, vd_ref, vu_ref, od_ref, ou_ref):
    def tile(t):
        return in_ref[t // 5, t % 5].astype(F32)

    for which, ref in enumerate((qd_ref, kd_ref, vd_ref, ou_ref)):
        for t in range(5):
            ref[:, t * 128 : (t + 1) * 128] = tile(which * 5 + t)
    for t in range(8):
        od_ref[:, t * 128 : (t + 1) * 128] = tile(20 + t)
        qu_ref[:, t * 128 : (t + 1) * 128] = tile(28 + t)
    ku_ref[...] = tile(36)
    vu_ref[...] = tile(37)


def shift(value, steps):
    count = lax.axis_size("ctx")
    first, last = max(0, -steps), min(count, count - steps)
    return lax.ppermute(value, "ctx", [(i, i + steps) for i in range(first, last)])


def exchange(value, groups):
    return lax.all_to_all(value, "ctx", 0, 0, tiled=True, axis_index_groups=groups)


def exchange_head(value):
    return lax.all_to_all(value, "head", 0, 0, tiled=True)


def after(value, *others):
    return lax.optimization_barrier((value, *others))[0]


def shards(x, q, keys, values, frozen, dout, lengths, qd, qu, kd, ku, vd, vu, od, ou):
    qd, kd, vd, od = qd.T, kd.T, vd.T, od.T
    wide = shaped((128, 1024), BF16)
    tall = shaped((1024, 128), BF16)
    block = shaped((2, 128, 128), BF16)
    pair = jnp.stack([keys, values])
    one = shift(pair, 4)
    low = call(project_kernel, shaped((8, 64, 128), BF16), x, dout, qd, kd, vd, ou)
    low = exchange_head(after(low, one))
    two, back = shift(one, 4), shift(jnp.stack([pair, one]), 12)
    window, x_rows, low = call(
        spread_kernel,
        (shaped((4, 4, 2, 128, 128), BF16), shaped((672, 128), BF16), shaped((64, 128), BF16)),
        pair, one, two, back, low, x,
    )
    window = exchange(window, Y_GROUPS)
    x_one = shift(x_rows, 4)
    x_two = shift(x_rows, 8)
    x_four, x_three = shift(x_two, 8), shift(x_two, 4)
    qs, qt, gs, gt, starts = call(
        prepare_kernel,
        (tall, wide, tall, wide, shaped((8, 128), F32)),
        q, frozen, low, od, lengths.reshape(1, 128),
    )
    dqt, ot, dkv = call(
        attention_kernel,
        (wide, wide, shaped((4, 4, 2, 128, 128), BF16)),
        qs, qt, gs, gt, window, starts,
        scratch=[
            pltpu.VMEM((4, 512, 1024), F32),
            pltpu.VMEM((2048, 1024), BF16),
            pltpu.VMEM((512, 128), F32),
            pltpu.VMEM((1, 1024), F32),
            pltpu.VMEM((1, 1024), F32),
        ],
        vmem=40,
        flops=3 << 30,
    )
    dkv = exchange(after(dkv, x_one, x_two), Y_GROUPS)
    dq, back, totals = call(
        finish_kernel,
        (wide, shaped((32, 128), BF16), shaped((16, 16, 128), BF16)),
        dqt, ot, low, od, qu,
    )
    parts, near, low_back = call(
        gather_kernel,
        (
            shaped((5, 2, 128, 128), BF16),
            shaped((2, 2, 128, 128), BF16),
            shaped((8, 192, 128), BF16),
        ),
        dkv, back, ku, vu,
    )
    near = shift(near, -4)
    low_back = exchange_head(after(low_back, x_four, x_three))
    low_back = after(low_back, near)
    packed = shaped((8, 5, 16, 128), BF16)
    sums = call(
        down_kernel, packed, low_back, x, x_one, x_two, x_three, x_four, dout, parts, low, totals
    )
    sums = call(sum_spread_kernel, packed, exchange(sums, EIGHTS))
    one_back, three_back = call(pass_kernel, (block, block), parts, near)
    three_back, one_back = shift(three_back, -12), shift(one_back, -4)
    sums = after(exchange(sums, STRIDED), three_back, one_back)
    sums = call(sum_spread_kernel, packed, sums)
    sums = exchange(sums, EIGHTS)
    dk, dv = call(
        owner_kernel,
        (shaped((128, 128), BF16), shaped((128, 128), BF16)),
        parts, one_back, three_back,
    )
    narrow, small = shaped((16, 640), F32), shaped((16, 128), F32)
    broad = shaped((16, 1024), F32)
    g_qd, g_qu, g_kd, g_ku, g_vd, g_vu, g_od, g_ou = call(
        unpack_kernel, (narrow, broad, narrow, small, narrow, small, broad, narrow), sums
    )
    return dq, dk, dv, g_qd.T, g_qu, g_kd.T, g_ku, g_vd.T, g_vu, g_od.T, g_ou


def solution(mesh):
    rows, cols, tokens = P("head", None), P(None, "head"), P("ctx", "head")
    return jax.shard_map(
        shards,
        mesh=mesh,
        in_specs=(tokens,) * 6 + (P(),) + (rows, cols) * 4,
        out_specs=(tokens,) * 3 + (rows, cols) * 4,
        check_vma=False,
    )
```

```python
import functools

import jax
import jax.numpy as jnp
from jax import lax
from jax.experimental import pallas as pl
from jax.experimental.pallas import tpu as pltpu
from jax.sharding import PartitionSpec as P

HEAD = 128
ROWS = 128
GROUP = 8
RANK = 16
TILES = 40
SCALE = HEAD**-0.5
LOG2E = 1.4426950408889634
ADAPTER_SCALE = 2.0
NEG = -1e30
F32 = jnp.float32
BF16 = jnp.bfloat16

Y_GROUPS = [[4 * z + y for y in range(4)] for z in range(16)]
EIGHTS = [[8 * g + i for i in range(8)] for g in range(8)]
STRIDED = [[g + 8 * i for i in range(8)] for g in range(8)]


def nn(a, b):
    return lax.dot_general(a, b, (((1,), (0,)), ((), ())), preferred_element_type=F32)


def nt(a, b):
    return lax.dot_general(a, b, (((1,), (1,)), ((), ())), preferred_element_type=F32)


def tn(a, b):
    return lax.dot_general(a, b, (((0,), (0,)), ((), ())), preferred_element_type=F32)


def call(body, outs, *args, scratch=(), vmem=32, flops=1 << 20):
    return pl.pallas_call(
        body,
        out_shape=outs,
        scratch_shapes=list(scratch),
        compiler_params=pltpu.CompilerParams(vmem_limit_bytes=vmem << 20),
        cost_estimate=pl.CostEstimate(flops=flops, bytes_accessed=1 << 20, transcendentals=0),
    )(*args)


def shaped(shape, dtype):
    return jax.ShapeDtypeStruct(shape, dtype)


def project_kernel(x_ref, dout_ref, qd_ref, kd_ref, vd_ref, ou_ref, out_ref):
    parts = [nt(ref[...], x_ref[...]) for ref in (qd_ref, kd_ref, vd_ref)]
    parts.append(nt(ou_ref[...], dout_ref[...]))
    low = jnp.concatenate(parts, axis=0).astype(BF16)
    for peer in range(8):
        out_ref[peer] = low


def spread_kernel(
    pair_ref, one_ref, two_ref, back_ref, low_ref, x_ref, out_ref, x_out, sum_ref
):
    y = lax.axis_index("ctx") % 4
    for dest in range(4):

        @pl.when(dest >= y)
        def _(dest=dest):
            out_ref[dest, 0] = pair_ref[...]

        @pl.when(dest < y)
        def _(dest=dest):
            out_ref[dest, 0] = back_ref[1]

        out_ref[dest, 1] = one_ref[...]
        out_ref[dest, 2] = two_ref[...]
        out_ref[dest, 3] = back_ref[0]
    low = low_ref[0].astype(F32)
    for peer in range(1, 8):
        low = low + low_ref[peer].astype(F32)
    low = low.astype(BF16)
    sum_ref[...] = low
    for t in range(5):
        x_out[t * 128 : (t + 1) * 128, :] = x_ref[:, t * 128 : (t + 1) * 128]
    x_out[640:672, :] = low[16:48]


def prepare_kernel(
    q_ref, f_ref, low_ref, od_ref, len_ref, qs_ref, qt_ref, gs_ref, gt_ref, start_ref
):
    doc = lax.broadcasted_iota(jnp.int32, (128, 128), 0)
    lane = lax.broadcasted_iota(jnp.int32, (128, 128), 1)
    lengths = jnp.broadcast_to(len_ref[...].astype(F32), (128, 128))
    ends = jnp.sum(jnp.where(lane <= doc, lengths, 0.0), axis=1, keepdims=True)
    position = (lane + lax.axis_index("ctx") * ROWS).astype(F32)
    start = jnp.max(jnp.where(ends <= position, ends, 0.0), axis=0, keepdims=True)
    start_ref[...] = jnp.broadcast_to(start, (8, 128))
    u = low_ref[48:64]
    for n in range(GROUP):
        cols = slice(n * HEAD, (n + 1) * HEAD)
        q_n = q_ref[:, cols]
        qs_ref[cols, :] = q_n
        qt_ref[:, cols] = q_n.T
        g_n = f_ref[:, cols].astype(F32) + ADAPTER_SCALE * tn(u, od_ref[:, cols])
        g_n = g_n.astype(BF16)
        gs_ref[cols, :] = g_n
        gt_ref[:, cols] = g_n.T


def attention_kernel(
    qs, qt, gs, gt, kv_ref, start_ref,
    dqt_ref, ot_ref, dkv_ref,
    s_ref, wide_low, bias, total, delta,
):
    index = lax.axis_index("ctx")
    y_place = index % 4
    start = start_ref[0:1]
    start = start.astype(jnp.int32)
    q_pos = lax.broadcasted_iota(jnp.int32, (1, 128), 1) + index * ROWS

    def keys(plane, which):
        return kv_ref[:, plane, which].reshape(512, HEAD)

    for plane in range(4):
        for y in range(4):
            back = (4 * plane + y_place - y) & 15
            k_pos = lax.broadcasted_iota(jnp.int32, (128, 128), 0) + (index - back) * ROWS
            bias[y * 128 : (y + 1) * 128, :] = jnp.where(
                (k_pos >= start) & (k_pos <= q_pos), 0.0, NEG
            )
        raw = nn(keys(plane, 0), qt[...])
        raw = raw * (SCALE * LOG2E) + jnp.concatenate([bias[...]] * GROUP, axis=1)
        s_ref[plane] = raw
        best = jnp.max(raw, axis=0, keepdims=True)
        peak = best if plane == 0 else jnp.maximum(peak, best)
    values_t = jnp.concatenate([keys(plane, 1).T for plane in range(4)], axis=1)
    norm = jnp.zeros((1, 1024), F32)
    for plane in range(4):
        prob = jnp.exp2(s_ref[plane] - peak)
        s_ref[plane] = prob
        norm = norm + jnp.sum(prob, axis=0, keepdims=True)
        wide_low[plane * 512 : plane * 512 + 512, :] = prob.astype(BF16)
    weighted = nn(values_t, wide_low[...])
    total[...] = 1.0 / norm
    for n in range(GROUP):
        cols = slice(n * HEAD, (n + 1) * HEAD)
        o_n = (weighted[:, cols] * total[:, cols]).astype(BF16)
        ot_ref[:, cols] = o_n
        delta[:, cols] = jnp.sum(
            o_n.astype(F32) * gt[:, cols].astype(F32), axis=0, keepdims=True
        )
    for plane in range(4):
        prob = s_ref[plane] * total[...]
        grad_prob = nn(keys(plane, 1), gt[...])
        grad_score = (prob * (grad_prob - delta[...])).astype(BF16)
        wide_low[plane * 512 : plane * 512 + 512, :] = grad_score
        dk = (nn(grad_score, qs[...]) * SCALE).astype(BF16)
        dv = nn(prob.astype(BF16), gs[...]).astype(BF16)
        dkv_ref[:, plane, 0] = dk.reshape(4, 128, HEAD)
        dkv_ref[:, plane, 1] = dv.reshape(4, 128, HEAD)
    keys_t = jnp.concatenate([keys(plane, 0).T for plane in range(4)], axis=1)
    dqt_ref[...] = (nn(keys_t, wide_low[...]) * SCALE).astype(BF16)


def finish_kernel(dqt_ref, ot_ref, low_ref, od_ref, qu_ref, dq_ref, back_ref, tot_ref):
    xa_q = low_ref[0:16]
    u = low_ref[48:64]
    out_adapter = jnp.zeros((RANK, ROWS), F32)
    back_q = jnp.zeros((RANK, ROWS), F32)
    for n in range(GROUP):
        cols = slice(n * HEAD, (n + 1) * HEAD)
        dq_t = dqt_ref[:, cols]
        dq_n = dq_t.T
        dq_ref[:, cols] = dq_n
        back_q = back_q + nn(qu_ref[:, cols], dq_t)
        tot_ref[GROUP + n] = (ADAPTER_SCALE * nn(xa_q, dq_n)).astype(BF16)
        o_n = ot_ref[:, cols]
        out_adapter = out_adapter + nn(od_ref[:, cols], o_n)
        tot_ref[n] = (ADAPTER_SCALE * nt(u, o_n)).astype(BF16)
    back_ref[0:16] = out_adapter.astype(BF16)
    back_ref[16:32] = back_q.astype(BF16)


def gather_kernel(y_ref, back_ref, ku_ref, vu_ref, part_ref, send_ref, out_ref):
    y = lax.axis_index("ctx") % 4
    parts = []
    for plane in range(5):
        term = [y_ref[source, plane % 4].astype(F32) for source in range(4)]
        if plane == 0:
            term = [term[source] * (source >= y).astype(F32) for source in range(4)]
        if plane == 4:
            term = [term[source] * (source < y).astype(F32) for source in range(4)]
        acc = (term[0] + term[1] + term[2] + term[3]).astype(BF16)
        part_ref[plane] = acc
        if plane in (2, 4):
            send_ref[plane // 2 - 1] = acc
        parts += [nt(ku_ref[...], acc[0]), nt(vu_ref[...], acc[1])]
    parts = jnp.concatenate(parts, axis=0).astype(BF16)
    for peer in range(8):
        out_ref[peer, 0:32] = back_ref[...]
        out_ref[peer, 32:192] = parts


def down_kernel(
    low_ref, x_ref, one_ref, two_ref, three_ref, four_ref, dout_ref, part_ref, sum_ref, tot_ref, out_ref
):
    low = low_ref[0].astype(F32)
    for peer in range(1, 8):
        low = low + low_ref[peer].astype(F32)
    low = low.astype(BF16)
    near = nn(low[16:64], x_ref[...])
    fars = (one_ref, two_ref, three_ref, four_ref)
    tiles = [near[0:16, t * 128 : (t + 1) * 128] for t in range(5)]
    down = []
    for t in range(5):
        acc = near[16:48, t * 128 : (t + 1) * 128]
        for p, far in enumerate(fars):
            acc = acc + nn(low[64 + 32 * p : 96 + 32 * p], far[t * 128 : (t + 1) * 128])
        down.append(acc)
    tiles += [acc[0:16] for acc in down] + [acc[16:32] for acc in down]
    up = nn(low[0:16], dout_ref[...])
    tiles += [up[:, t * 128 : (t + 1) * 128] for t in range(5)]
    tiles = [(ADAPTER_SCALE * tile).astype(BF16) for tile in tiles]
    tiles += [tot_ref[t] for t in range(16)]
    for which in range(2):
        rows = slice(16 * which, 16 * which + 16)
        acc = nn(sum_ref[16 + 16 * which : 32 + 16 * which], part_ref[0, which])
        for p, far in enumerate(fars):
            acc = acc + nn(far[640 + rows.start : 640 + rows.stop], part_ref[p + 1, which])
        tiles.append((ADAPTER_SCALE * acc).astype(BF16))
    zero = jnp.zeros((16, 128), BF16)
    tiles += [zero, zero]
    for t, tile in enumerate(tiles):
        out_ref[t // 5, t % 5] = tile


def pass_kernel(part_ref, near_ref, three_ref, one_ref):
    one_ref[...] = (part_ref[1].astype(F32) + near_ref[0].astype(F32)).astype(BF16)
    three_ref[...] = (part_ref[3].astype(F32) + near_ref[1].astype(F32)).astype(BF16)


def owner_kernel(part_ref, one_ref, three_ref, dk_ref, dv_ref):
    for which, ref in enumerate((dk_ref, dv_ref)):
        acc = part_ref[0, which].astype(F32) + one_ref[which].astype(F32)
        ref[...] = (acc + three_ref[which].astype(F32)).astype(BF16)


def sum_spread_kernel(in_ref, out_ref):
    acc = in_ref[0].astype(F32)
    for peer in range(1, 8):
        acc = acc + in_ref[peer].astype(F32)
    acc = acc.astype(BF16)
    for peer in range(8):
        out_ref[peer] = acc


def unpack_kernel(in_ref, qd_ref, qu_ref, kd_ref, ku_ref, vd_ref, vu_ref, od_ref, ou_ref):
    def tile(t):
        return in_ref[t // 5, t % 5].astype(F32)

    for which, ref in enumerate((qd_ref, kd_ref, vd_ref, ou_ref)):
        for t in range(5):
            ref[:, t * 128 : (t + 1) * 128] = tile(which * 5 + t)
    for t in range(8):
        od_ref[:, t * 128 : (t + 1) * 128] = tile(20 + t)
        qu_ref[:, t * 128 : (t + 1) * 128] = tile(28 + t)
    ku_ref[...] = tile(36)
    vu_ref[...] = tile(37)


def shift(value, steps):
    count = lax.axis_size("ctx")
    first, last = max(0, -steps), min(count, count - steps)
    return lax.ppermute(value, "ctx", [(i, i + steps) for i in range(first, last)])


def exchange(value, groups):
    return lax.all_to_all(value, "ctx", 0, 0, tiled=True, axis_index_groups=groups)


def exchange_head(value):
    return lax.all_to_all(value, "head", 0, 0, tiled=True)


def after(value, *others):
    return lax.optimization_barrier((value, *others))[0]


def shards(x, q, keys, values, frozen, dout, lengths, qd, qu, kd, ku, vd, vu, od, ou):
    qd, kd, vd, od = qd.T, kd.T, vd.T, od.T
    wide = shaped((128, 1024), BF16)
    tall = shaped((1024, 128), BF16)
    block = shaped((2, 128, 128), BF16)
    pair = jnp.stack([keys, values])
    one = shift(pair, 4)
    low = call(project_kernel, shaped((8, 64, 128), BF16), x, dout, qd, kd, vd, ou)
    low = exchange_head(after(low, one))
    two, back = shift(one, 4), shift(jnp.stack([pair, one]), 12)
    window, x_rows, low = call(
        spread_kernel,
        (shaped((4, 4, 2, 128, 128), BF16), shaped((672, 128), BF16), shaped((64, 128), BF16)),
        pair, one, two, back, low, x,
    )
    window = exchange(window, Y_GROUPS)
    x_one = shift(x_rows, 4)
    x_two = shift(x_rows, 8)
    x_four, x_three = shift(x_two, 8), shift(x_two, 4)
    qs, qt, gs, gt, starts = call(
        prepare_kernel,
        (tall, wide, tall, wide, shaped((8, 128), F32)),
        q, frozen, low, od, lengths.reshape(1, 128),
    )
    dqt, ot, dkv = call(
        attention_kernel,
        (wide, wide, shaped((4, 4, 2, 128, 128), BF16)),
        qs, qt, gs, gt, window, starts,
        scratch=[
            pltpu.VMEM((4, 512, 1024), F32),
            pltpu.VMEM((2048, 1024), BF16),
            pltpu.VMEM((512, 128), F32),
            pltpu.VMEM((1, 1024), F32),
            pltpu.VMEM((1, 1024), F32),
        ],
        vmem=40,
        flops=3 << 30,
    )
    dkv = exchange(after(dkv, x_one, x_two), Y_GROUPS)
    dq, back, totals = call(
        finish_kernel,
        (wide, shaped((32, 128), BF16), shaped((16, 16, 128), BF16)),
        dqt, ot, low, od, qu,
    )
    parts, near, low_back = call(
        gather_kernel,
        (
            shaped((5, 2, 128, 128), BF16),
            shaped((2, 2, 128, 128), BF16),
            shaped((8, 192, 128), BF16),
        ),
        dkv, back, ku, vu,
    )
    near = shift(near, -4)
    low_back = exchange_head(after(low_back, x_four, x_three))
    low_back = after(low_back, near)
    packed = shaped((8, 5, 16, 128), BF16)
    sums = call(
        down_kernel, packed, low_back, x, x_one, x_two, x_three, x_four, dout, parts, low, totals
    )
    sums = call(sum_spread_kernel, packed, exchange(sums, EIGHTS))
    three_back, one_back = call(pass_kernel, (block, block), parts, near)
    three_back, one_back = shift(three_back, -12), shift(one_back, -4)
    sums = after(exchange(sums, STRIDED), three_back, one_back)
    sums = call(sum_spread_kernel, packed, sums)
    sums = exchange(sums, EIGHTS)
    dk, dv = call(
        owner_kernel,
        (shaped((128, 128), BF16), shaped((128, 128), BF16)),
        parts, three_back, one_back,
    )
    narrow, small = shaped((16, 640), F32), shaped((16, 128), F32)
    broad = shaped((16, 1024), F32)
    g_qd, g_qu, g_kd, g_ku, g_vd, g_vu, g_od, g_ou = call(
        unpack_kernel, (narrow, broad, narrow, small, narrow, small, broad, narrow), sums
    )
    return dq, dk, dv, g_qd.T, g_qu, g_kd.T, g_ku, g_vd.T, g_vu, g_od.T, g_ou


def solution(mesh):
    rows, cols, tokens = P("head", None), P(None, "head"), P("ctx", "head")
    return jax.shard_map(
        shards,
        mesh=mesh,
        in_specs=(tokens,) * 6 + (P(),) + (rows, cols) * 4,
        out_specs=(tokens,) * 3 + (rows, cols) * 4,
        check_vma=False,
    )
```
